128 devices in a mesh: dp: 32 (over z, y, core), hid: 4 (over x).
Axes of the slice: x: 4, y: 4, z: 4, core: 2. Of those that a mesh axis runs over, the one named last changes fastest.
Arguments:
- gate_pre: bfloat16 [4096, 2, 8192], P('dp', None, 'hid'), may hold values from -6 to 6
- up_pre: bfloat16 [4096, 2, 8192], P('dp', None, 'hid'), may hold values from -6 to 6
- out_grad: bfloat16 [4096, 6144], P('dp'), may hold values from -6 to 6
- combine: float32 [4096, 2], P('dp'), may hold values from 0.1 to 0.9
- expert_ids: int32 [4096, 2], P('dp'), may hold values from 0 to 7, all different within a row; in each aligned block of 128 rows (0 to 127, 128 to 255, ...) at most 48 rows name the same one
- down_weight: bfloat16 [32, 8192, 1536], P('dp', 'hid'), may hold values from -0.0625 to 0.0625
Outputs:
- mixed: bfloat16 [4096, 4, 1536], P('dp', None, 'hid')
- combine_grad: float32 [4096, 2], P('dp')
- gate_grad: bfloat16 [4096, 2, 8192], P('dp', None, 'hid')
- up_grad: bfloat16 [4096, 2, 8192], P('dp', None, 'hid')
- weight_grad: bfloat16 [32, 8192, 1536], P('dp', 'hid')
The draws below stay inside these ranges and needn't reach their ends.
Inputs may be any that keep to these rules, and one draw needn't show every extreme that they name: `expert_ids`: each token names two different experts. Among the 128 tokens of one dp index no expert is named by more than 48 tokens, and in every draw some expert is named by exactly 48 of them.
All inputs are finite; a program needn't handle non-finite values.
Results may differ from the reference program's by a relative error of at most 0.0057.
Values may be sent and summed in bfloat16 or wider, within the bound.
A program may use at most 448 MiB of HBM per device.

```python
import math
import jax
import jax.numpy as jnp
import numpy as np
from jax import lax

D = 6144
FF = 8192
E = 8
TOP = 2
TOK_DEV = 128
CAP = 48
TOKENS = 4096
SLICES = 4
SLICE = 1536
N_DP = 32


def level_of(own_key, shape, shards, smallest, high):
    def one(axis_at, blocks):
        draws = jax.random.uniform(jax.random.fold_in(jax.random.fold_in(own_key, 6), axis_at), (blocks,), jnp.float32, smallest / len(shards), high / len(shards))
        return jnp.repeat(jnp.exp(draws), shape[axis_at] // blocks).reshape((-1,) + (1,) * (len(shape) - axis_at - 1))

    loudness = one(*shards[0])
    for cut in shards[1:]:
        loudness = loudness * one(*cut)
    return loudness


def deal_out(rng, own, number, rows, count, top, bound, skew):
    order = jax.random.permutation(rng, count)
    packed, usual = shares(count, rows * top, bound, skew, True), shares(count, rows * top, bound, skew, False)
    places = jnp.arange(count)

    def named(lengths, rotation):
        used = int((lengths > 0).sum())
        fixed = max(1, used // 4)
        moved = fixed + (places - fixed + rotation * (used - fixed)) % max(1, count - fixed)
        return jnp.zeros((count,), jnp.int32).at[order[jnp.where(places < fixed, places, moved)]].set(jnp.asarray(lengths, jnp.int32))

    lengths = jnp.where(number % 4 == 0, named(packed, number // 4), named(usual, number - number // 4 - 1))
    mixed = jax.random.permutation(jax.random.fold_in(own, 3), count)
    giver, sink = mixed[0:count // 2 * 2:2], mixed[1:count // 2 * 2:2]
    room = jnp.minimum(lengths[giver] - 1, bound - lengths[sink]) // 2
    room = jnp.where((giver == order[0]) | (sink == order[0]) | (lengths[sink] == 0), 0, jnp.maximum(room, 0))
    moved = jax.random.randint(jax.random.fold_in(own, 4), (count // 2,), 0, 1 << 20) % (room + 1)
    lengths = lengths.at[giver].add(-moved).at[sink].add(moved)
    labels = jnp.searchsorted(jnp.cumsum(lengths), jnp.arange(rows * top), side="right").astype(jnp.int32)
    table = labels.reshape(top, rows).T
    table = table[jax.random.permutation(jax.random.fold_in(own, 1), rows)]
    rotation = jax.random.randint(jax.random.fold_in(own, 2), (rows, 1), 0, top)
    return jnp.take_along_axis(table, (jnp.arange(top)[None, :] + rotation) % top, axis=1)


def shares(count, total, most, slope, full):
    portions = [(1 << 20) // math.isqrt(standing ** slope) + 1 for standing in range(1, count + 1)]
    largest = most if full else min(most, max(-(-total // count), total * portions[0] // sum(portions)))
    least = 1 if total - largest >= count - 1 else 0
    given, rest = [largest] + [least] * (count - 1), total - largest - least * (count - 1)
    while rest > 0:
        free = [i for i in range(1, count) if given[i] < largest] or [i for i in range(1, count) if given[i] < most]
        mass, left = sum([portions[i] for i in free]), rest
        for i in free:
            addition = min(most - given[i], max(1, left * portions[i] // mass), rest)
            given[i] = given[i] + addition
            rest = rest - addition
    return np.array(given)


def centred(stream_key, dims, scale, reach, cuts=(), held_as=jnp.bfloat16):
    array = jax.random.normal(stream_key, dims, jnp.float32) * scale
    if len(cuts) > 0:
        array = level_of(stream_key, dims, cuts, -0.22, 0.18) * array
    return jnp.clip(array, min=-reach, max=reach).astype(held_as)


def setup_inputs(seed: int = 0) -> dict:
    keys = jax.random.split(jax.random.key(seed), 7)
    gate_pre = centred(keys[0], (TOKENS, TOP, FF), 1.0, 6.0, ((0, 32), (2, 4)))
    up_pre = centred(keys[1], (TOKENS, TOP, FF), 1.0, 6.0, ((0, 32), (2, 4)))
    out_grad = centred(keys[2], (TOKENS, D), 1.0, 6.0, ((0, 32),))
    combine = jnp.clip(0.1 + 0.79999997 * jax.random.uniform(keys[3], (TOKENS, TOP), jnp.float32) ** level_of(keys[3], (TOKENS, TOP), ((0, 32),), -0.2, 0.2), 0.1, 0.9)
    expert_ids_keys = jax.random.split(jax.random.fold_in(keys[4], 1), TOKENS // TOK_DEV)
    expert_ids_turns = jax.random.permutation(jax.random.fold_in(keys[4], 3), TOKENS // TOK_DEV)
    expert_ids = jax.vmap(lambda own, number: deal_out(jax.random.fold_in(keys[4], 2), own, number, TOK_DEV, E, TOP, CAP, 2))(expert_ids_keys, expert_ids_turns).reshape((TOKENS, TOP))
    down_weight = centred(keys[5], (E * SLICES, FF, SLICE), FF ** -0.5, 0.0625, ((0, 32), (1, 4)))
    return {"gate_pre": gate_pre, "up_pre": up_pre, "out_grad": out_grad, "combine": combine, "expert_ids": expert_ids, "down_weight": down_weight}


def reference(gate_pre, up_pre, out_grad, combine, expert_ids, down_weight):
    slices = N_DP // E
    slice_width = D // slices
    capacity = CAP
    gate_f = gate_pre.astype(jnp.float32)
    up_f = up_pre.astype(jnp.float32)
    sigmoid_gate = jax.nn.sigmoid(gate_f)
    hidden = (gate_f * sigmoid_gate * up_f).astype(jnp.bfloat16)
    scaled = (combine[:, :, None] * out_grad[:, None, :].astype(jnp.float32)).astype(jnp.bfloat16)
    blocked = expert_ids.reshape(N_DP, TOK_DEV * TOP)
    onehot = (blocked[:, :, None] == jnp.arange(E, dtype=jnp.int32)[None, None, :]).astype(jnp.int32)
    earlier = jnp.cumsum(onehot, axis=1) - onehot
    position = jnp.sum(earlier * onehot, axis=2).astype(jnp.int32)
    device_row = jnp.arange(N_DP, dtype=jnp.int32)[:, None]
    place = ((blocked * N_DP + device_row) * capacity + position).reshape(-1).astype(jnp.int32)
    rows_all = E * N_DP * capacity
    hidden_buf = jnp.zeros((rows_all, FF), jnp.bfloat16).at[place].set(hidden.reshape(-1, FF))
    grad_buf = jnp.zeros((rows_all, D), jnp.bfloat16).at[place].set(scaled.reshape(-1, D))
    hidden_buf = hidden_buf.reshape(E, N_DP * capacity, FF)
    grad_buf = grad_buf.reshape(E, N_DP * capacity, D)
    weights = down_weight.reshape(E, slices, FF, slice_width).transpose(0, 2, 1, 3).reshape(E, FF, D)

    def per_expert(items):
        hid_rows, grad_rows, matrix = items
        outputs = jnp.dot(hid_rows, matrix, preferred_element_type=jnp.float32)
        back = lax.dot_general(grad_rows, matrix, (((1,), (1,)), ((), ())), preferred_element_type=jnp.float32)
        wgrad = lax.dot_general(hid_rows, grad_rows, (((0,), (0,)), ((), ())), preferred_element_type=jnp.float32)
        return outputs, back, wgrad.astype(jnp.bfloat16)

    outputs, backs, wgrads = lax.map(per_expert, (hidden_buf, grad_buf, weights))
    slot_out = outputs.reshape(-1, D)[place].reshape(TOKENS, TOP, D)
    hidden_grad = backs.reshape(-1, FF)[place].reshape(TOKENS, TOP, FF)
    mixed = jnp.sum(combine[:, :, None] * slot_out, axis=1).astype(jnp.bfloat16).reshape(TOKENS, slices, slice_width)
    combine_grad = jnp.sum(out_grad.astype(jnp.float32)[:, None, :] * slot_out, axis=2)
    gate_grad = (hidden_grad * up_f * sigmoid_gate * (1.0 + gate_f * (1.0 - sigmoid_gate))).astype(jnp.bfloat16)
    up_grad = (hidden_grad * gate_f * sigmoid_gate).astype(jnp.bfloat16)
    weight_grad = wgrads.reshape(E, FF, slices, slice_width).transpose(0, 2, 1, 3).reshape(E * slices, FF, slice_width)
    return mixed, combine_grad, gate_grad, up_grad, weight_grad
```

```python
import jax
import jax.numpy as jnp
from jax import lax
from jax.experimental import pallas as pl
from jax.experimental.pallas import tpu as pltpu
from jax.sharding import PartitionSpec as P

E = 8
TOP = 2
CAP = 48
F32 = jnp.float32
BF16 = jnp.bfloat16
MESH = pl.DeviceIdType.MESH


def exchange_kernel(
    hs, gs, w, oh, bh, wg, cg,
    hr, gr, os, orx, od, bs, br, wt, cgs, cgr,
    send_h, send_g, recv_h, recv_g, xg_send, xg_recv, sib_send, sib_recv,
    xo_send, xo_recv, bsib_send, bsib_recv, home_o_send, home_b_send,
    home_recv, wg_sem, cg_send, cg_recv,
):
    me = lax.axis_index("dp")
    x = lax.axis_index("hid")
    z = lax.div(me, 8)
    yc = lax.rem(me, 8)
    core = lax.rem(me, 2)
    e_me = lax.div(me, 4)
    j_me = lax.rem(me, 4)
    sibling = me + 1 - 2 * core
    rows_n = 8 * CAP
    q_w = gr.shape[1] // 4
    half_w = hr.shape[1] // 2

    def m(v, k):
        return pl.multiple_of(v, k)

    barrier = pltpu.get_barrier_semaphore()

    def greet_dp(n, carry):
        peer = lax.rem(me + n, 32)
        pl.semaphore_signal(barrier, inc=1, device_id=(peer, x), device_id_type=MESH)
        return carry

    lax.fori_loop(1, 32, greet_dp, 0)
    for o in range(1, 4):
        pl.semaphore_signal(
            barrier, inc=1, device_id=(me, lax.rem(x + o, 4)), device_id_type=MESH
        )
    pl.semaphore_wait(barrier, 34)

    my_half = m(core * half_w, 128)
    other_half = m((1 - core) * half_w, 128)
    my_quarter = m(x * q_w, 128)
    my_rows = m(me * CAP, 16)
    my_expert_rows = m(e_me * CAP, 16)

    def base_of(r):
        return m(lax.rem(z - r + 4, 4) * rows_n, 16)

    def partner(n):
        return lax.rem(z + lax.div(n, 8), 4) * 8 + lax.rem(yc + lax.rem(n, 8), 8)

    pltpu.make_async_copy(
        gs.at[pl.ds(my_expert_rows, CAP), pl.ds(m(j_me * q_w, 128), q_w)],
        gr.at[pl.ds(my_rows, CAP), pl.ds(my_quarter, q_w)],
        recv_g.at[0],
    ).start()
    pltpu.make_async_copy(
        hs.at[pl.ds(my_expert_rows, CAP), pl.ds(my_half, half_w)],
        hr.at[pl.ds(my_rows, CAP), pl.ds(my_half, half_w)],
        recv_h.at[0],
    ).start()

    def g_copy(n):
        p = partner(n)
        return pltpu.make_async_remote_copy(
            src_ref=gs.at[
                pl.ds(m(lax.div(p, 4) * CAP, 16), CAP), pl.ds(m(lax.rem(p, 4) * q_w, 128), q_w)
            ],
            dst_ref=gr.at[pl.ds(my_rows, CAP), pl.ds(my_quarter, q_w)],
            send_sem=send_g.at[n],
            recv_sem=recv_g.at[lax.div(n, 8)],
            device_id=(p, x),
            device_id_type=MESH,
        )

    def h_copy(n):
        p = partner(n)
        cols = pl.ds(m(lax.rem(p, 2) * half_w, 128), half_w)
        return pltpu.make_async_remote_copy(
            src_ref=hs.at[pl.ds(m(lax.div(p, 4) * CAP, 16), CAP), cols],
            dst_ref=hr.at[pl.ds(my_rows, CAP), cols],
            send_sem=send_h.at[n],
            recv_sem=recv_h.at[lax.div(n, 8)],
            device_id=(p, x),
            device_id_type=MESH,
        )

    def loop(lo, hi, f):
        def step(n, carry):
            f(n)
            return carry

        lax.fori_loop(lo, hi, step, 0)

    loop(1, 32, lambda n: g_copy(n).start())
    loop(1, 32, lambda n: h_copy(n).start())

    def xg_copy(r, o):
        part = gr.at[pl.ds(base_of(r), rows_n), pl.ds(my_quarter, q_w)]
        return pltpu.make_async_remote_copy(
            src_ref=part, dst_ref=part,
            send_sem=xg_send.at[r, o - 1], recv_sem=xg_recv.at[r, o - 1],
            device_id=(me, lax.rem(x + o, 4)), device_id_type=MESH,
        )

    def xg_wait(r, o):
        cols = m(lax.rem(x - o + 4, 4) * q_w, 128)
        part = gr.at[pl.ds(base_of(r), rows_n), pl.ds(cols, q_w)]
        pltpu.make_async_copy(part, part, xg_recv.at[r, o - 1]).wait()

    def pass_g(r):
        part = gr.at[pl.ds(base_of(r), rows_n), pl.ds(my_quarter, q_w)]
        pltpu.make_async_copy(part, part, recv_g.at[r]).wait()
        for o in range(1, 4):
            xg_copy(r, o).start()

    loop(0, 4, pass_g)

    def sib_copy(r):
        part = hr.at[pl.ds(base_of(r), rows_n), pl.ds(my_half, half_w)]
        return pltpu.make_async_remote_copy(
            src_ref=part, dst_ref=part, send_sem=sib_send.at[r], recv_sem=sib_recv.at[r],
            device_id=(sibling, x), device_id_type=MESH,
        )

    def pass_h(r):
        part = hr.at[pl.ds(base_of(r), rows_n), pl.ds(my_half, half_w)]
        pltpu.make_async_copy(part, part, recv_h.at[r]).wait()
        sib_copy(r).start()

    def xo_copy(r, o):
        peer = lax.rem(x + o, 4)
        return pltpu.make_async_remote_copy(
            src_ref=os.at[pl.ds(base_of(r), rows_n), pl.ds(m(peer * q_w, 128), q_w)],
            dst_ref=orx.at[o - 1, pl.ds(base_of(r), rows_n), :],
            send_sem=xo_send.at[r, o - 1], recv_sem=xo_recv.at[r, o - 1],
            device_id=(me, peer), device_id_type=MESH,
        )

    def out_product(r):
        part = hr.at[pl.ds(base_of(r), rows_n), pl.ds(other_half, half_w)]
        pltpu.make_async_copy(part, part, sib_recv.at[r]).wait()
        rows = pl.ds(base_of(r), rows_n)

        def tile(q):
            cols = pl.ds(m(q * 2 * q_w, 128), 2 * q_w)
            acc = jnp.dot(hr[rows, :], w[:, cols], preferred_element_type=F32)
            os[rows, cols] = acc.astype(BF16)

        loop(0, 2, tile)
        for o in range(1, 4):
            xo_copy(r, o).start()

    pass_h(0)

    def h_step(r):
        pass_h(r + 1)
        out_product(r)

    loop(0, 3, h_step)
    out_product(3)

    def bsib_copy(r):
        rows = pl.ds(base_of(r), rows_n)
        return pltpu.make_async_remote_copy(
            src_ref=bs.at[rows, pl.ds(other_half, half_w)],
            dst_ref=br.at[rows, :],
            send_sem=bsib_send.at[r], recv_sem=bsib_recv.at[r],
            device_id=(sibling, x), device_id_type=MESH,
        )

    def back_product(r):
        for o in range(1, 4):
            xg_wait(r, o)
        rows = pl.ds(base_of(r), rows_n)

        def tile(n):
            cols = pl.ds(m(n * 512, 128), 512)
            acc = lax.dot_general(
                gr[rows, :], w[cols, :], (((1,), (1,)), ((), ())), preferred_element_type=F32
            )
            bs[rows, cols] = acc.astype(BF16)

        loop(0, 4, tile)
        bsib_copy(r).start()

    def home_b_copy(n):
        p = lax.rem(z - lax.div(n, 8) + 4, 4) * 8 + lax.rem(yc + lax.rem(n, 8), 8)
        return pltpu.make_async_remote_copy(
            src_ref=br.at[pl.ds(m(p * CAP, 16), CAP), :],
            dst_ref=bh.at[
                pl.ds(m((lax.div(j_me, 2) * E + e_me) * CAP, 16), CAP), pl.ds(my_half, half_w)
            ],
            send_sem=home_b_send.at[n], recv_sem=home_recv.at[1],
            device_id=(p, x), device_id_type=MESH,
        )

    def home_o_copy(n):
        p = lax.rem(z - lax.div(n, 8) + 4, 4) * 8 + lax.rem(yc + lax.rem(n, 8), 8)
        return pltpu.make_async_remote_copy(
            src_ref=od.at[pl.ds(m(p * CAP, 16), CAP), :],
            dst_ref=oh.at[pl.ds(my_expert_rows, CAP), pl.ds(m(j_me * q_w, 128), q_w)],
            send_sem=home_o_send.at[n], recv_sem=home_recv.at[0],
            device_id=(p, x), device_id_type=MESH,
        )

    def back_sum(r):
        rows = pl.ds(base_of(r), rows_n)
        part = br.at[rows, :]
        pltpu.make_async_copy(part, part, bsib_recv.at[r]).wait()

        def tile(i):
            sub = pl.ds(m(base_of(r) + i * CAP, 16), CAP)
            total = br[sub, :].astype(F32) + bs[sub, pl.ds(my_half, half_w)].astype(F32)
            br[sub, :] = total.astype(BF16)

        loop(0, 8, tile)

    def out_sum(r):
        for o in range(1, 4):
            part = orx.at[o - 1, pl.ds(base_of(r), rows_n), :]
            pltpu.make_async_copy(part, part, xo_recv.at[r, o - 1]).wait()

        def tile(i):
            sub = pl.ds(m(base_of(r) + i * CAP, 16), CAP)
            total = os[sub, pl.ds(my_quarter, q_w)].astype(F32)
            for k in range(3):
                total = total + orx[k, sub, :].astype(F32)
            od[sub, :] = total.astype(BF16)

        loop(0, 8, tile)

    def back_first():
        back_sum(0)
        pltpu.make_async_copy(
            br.at[pl.ds(my_rows, CAP), :],
            bh.at[
                pl.ds(m((lax.div(j_me, 2) * E + e_me) * CAP, 16), CAP), pl.ds(my_half, half_w)
            ],
            home_recv.at[1],
        ).start()
        loop(1, 8, lambda n: home_b_copy(n).start())

    def back_next(r):
        back_sum(r)
        loop(r * 8, r * 8 + 8, lambda n: home_b_copy(n).start())

    back_product(0)
    back_product(1)
    back_first()

    def b_step(r):
        back_product(r + 1)
        back_next(r)

    loop(1, 3, b_step)
    back_next(3)

    def wg_copy(n):
        rows = pl.ds(m(n * 256, 16), 256)
        return pltpu.make_async_copy(wt.at[rows, :], wg.at[rows, :], wg_sem.at[n])

    def wg_tile(n):
        cols = pl.ds(m(n * 256, 128), 256)
        acc = lax.dot_general(
            hr[:, cols], gr[...], (((0,), (0,)), ((), ())), preferred_element_type=F32
        )
        wt[pl.ds(m(n * 256, 16), 256), :] = acc.astype(BF16)
        wg_copy(n).start()

    def out_first():
        out_sum(0)
        pltpu.make_async_copy(
            od.at[pl.ds(my_rows, CAP), :],
            oh.at[pl.ds(my_expert_rows, CAP), pl.ds(m(j_me * q_w, 128), q_w)],
            home_recv.at[0],
        ).start()
        loop(1, 8, lambda n: home_o_copy(n).start())

    def out_next(r):
        out_sum(r)
        loop(r * 8, r * 8 + 8, lambda n: home_o_copy(n).start())

    loop(0, 8, wg_tile)
    out_first()
    loop(1, 4, out_next)

    pltpu.make_async_copy(oh, oh, home_recv.at[0]).wait()
    fold = jnp.zeros((rows_n, 128), F32)
    for k in range(4 * q_w // 128):
        cols = slice(k * 128, (k + 1) * 128)
        fold = fold + oh[:, cols].astype(F32) * gs[:, cols].astype(F32)
    high = fold.astype(BF16)
    low = (fold - high.astype(F32)).astype(BF16)
    ones = jnp.ones((8, 128), BF16)
    last = (((1,), (1,)), ((), ()))
    cgs[...] = lax.dot_general(ones, high, last, preferred_element_type=F32) + lax.dot_general(
        ones, low, last, preferred_element_type=F32
    )

    def cg_copy(o):
        return pltpu.make_async_remote_copy(
            src_ref=cgs, dst_ref=cgr.at[o - 1],
            send_sem=cg_send.at[o - 1], recv_sem=cg_recv.at[o - 1],
            device_id=(me, lax.rem(x + o, 4)), device_id_type=MESH,
        )

    for o in range(1, 4):
        cg_copy(o).start()
    for o in range(1, 4):
        cg_copy(o).wait_recv()
    cg[...] = cgs[...] + cgr[0] + cgr[1] + cgr[2]

    pltpu.make_async_copy(bh, bh, home_recv.at[1]).wait()
    for o in range(1, 4):
        cg_copy(o).wait_send()
    loop(0, 8, lambda n: wg_copy(n).wait())

    def drain(n):
        g_copy(n).wait_send()
        h_copy(n).wait_send()
        home_b_copy(n).wait_send()
        home_o_copy(n).wait_send()

    loop(1, 32, drain)

    def drain_r(r):
        sib_copy(r).wait_send()
        bsib_copy(r).wait_send()
        for o in range(1, 4):
            xg_copy(r, o).wait_send()
            xo_copy(r, o).wait_send()

    loop(0, 4, drain_r)


def exchange(hs, gs, w):
    rows, ff = hs.shape
    width = gs.shape[1]
    rows_all = 32 * CAP
    vmem = pl.BlockSpec(memory_space=pltpu.VMEM)
    dma = pltpu.SemaphoreType.DMA
    return pl.pallas_call(
        exchange_kernel,
        out_shape=(
            jax.ShapeDtypeStruct((rows, width), BF16),
            jax.ShapeDtypeStruct((2 * rows, ff), BF16),
            jax.ShapeDtypeStruct((ff, width), BF16),
            jax.ShapeDtypeStruct((8, rows), F32),
        ),
        in_specs=[vmem] * 3,
        out_specs=(vmem, vmem, pl.BlockSpec(memory_space=pl.ANY), vmem),
        scratch_shapes=[
            pltpu.VMEM((rows_all, ff), BF16),
            pltpu.VMEM((rows_all, width), BF16),
            pltpu.VMEM((rows_all, width), BF16),
            pltpu.VMEM((3, rows_all, width // 4), BF16),
            pltpu.VMEM((rows_all, width // 4), BF16),
            pltpu.VMEM((rows_all, ff), BF16),
            pltpu.VMEM((rows_all, ff // 2), BF16),
            pltpu.VMEM((ff, width), BF16),
            pltpu.VMEM((8, rows), F32),
            pltpu.VMEM((3, 8, rows), F32),
            dma((32,)), dma((32,)), dma((4,)), dma((4,)),
            dma((4, 3)), dma((4, 3)), dma((4,)), dma((4,)),
            dma((4, 3)), dma((4, 3)), dma((4,)), dma((4,)),
            dma((32,)), dma((32,)), dma((2,)), dma((8,)), dma((3,)), dma((3,)),
        ],
        compiler_params=pltpu.CompilerParams(
            collective_id=0, has_side_effects=True, vmem_limit_bytes=62 * 1024 * 1024
        ),
        cost_estimate=pl.CostEstimate(
            flops=6 * rows_all * ff * width, bytes_accessed=30000000, transcendentals=0
        ),
    )(hs, gs, w)


def per_device(gate_pre, up_pre, out_grad, combine, expert_ids, down_weight):
    tokens = gate_pre.shape[0]
    x = lax.axis_index("hid")
    width = down_weight.shape[2]
    quarter = width // 4
    rows = E * CAP
    flat = jnp.concatenate([expert_ids[:, 0], expert_ids[:, 1]])
    onehot = (flat[:, None] == jnp.arange(E, dtype=jnp.int32)[None, :]).astype(BF16)
    count = tokens * TOP
    before = (jnp.arange(count)[:, None] > jnp.arange(count)[None, :]).astype(BF16)
    earlier = jnp.dot(before, onehot, preferred_element_type=F32)
    position = jnp.sum(earlier * onehot.astype(F32), axis=1).astype(jnp.int32)
    target = flat * CAP + position
    row_ids = jnp.arange(rows, dtype=jnp.int32)
    pack = (target[None, :] == row_ids[:, None]).astype(BF16)
    hit = target[:, None] == row_ids[None, :]
    unpack = hit.astype(BF16)

    gate_f = gate_pre.astype(F32)
    up_f = up_pre.astype(F32)
    sig = jax.nn.sigmoid(gate_f)
    hidden = (gate_f * sig * up_f).astype(BF16)
    hs = (
        jnp.dot(pack[:, :tokens], hidden[:, 0], preferred_element_type=F32)
        + jnp.dot(pack[:, tokens:], hidden[:, 1], preferred_element_type=F32)
    ).astype(BF16)
    mine = jnp.concatenate(
        [
            lax.dynamic_slice_in_dim(out_grad, j * width + x * quarter, quarter, axis=1)
            for j in range(4)
        ],
        axis=1,
    ).astype(F32)
    scaled0 = (combine[:, 0:1] * mine).astype(BF16)
    scaled1 = (combine[:, 1:2] * mine).astype(BF16)
    gs = (
        jnp.dot(pack[:, :tokens], scaled0, preferred_element_type=F32)
        + jnp.dot(pack[:, tokens:], scaled1, preferred_element_type=F32)
    ).astype(BF16)

    oh, bh, wg, cg = exchange(hs, gs, down_weight[0])

    mixed = (
        combine[:, 0:1] * jnp.dot(unpack[:tokens], oh, preferred_element_type=F32)
        + combine[:, 1:2] * jnp.dot(unpack[tokens:], oh, preferred_element_type=F32)
    ).astype(BF16).reshape(tokens, 4, quarter)
    slot_cg = jnp.sum(jnp.where(hit, cg[0:1, :], 0.0), axis=1)
    combine_grad = jnp.stack([slot_cg[:tokens], slot_cg[tokens:]], axis=1) / combine
    both = jnp.concatenate([unpack, unpack], axis=1)
    hidden_grad = jnp.stack(
        [
            jnp.dot(both[:tokens], bh, preferred_element_type=F32),
            jnp.dot(both[tokens:], bh, preferred_element_type=F32),
        ],
        axis=1,
    )
    gate_grad = (hidden_grad * up_f * sig * (1.0 + gate_f * (1.0 - sig))).astype(BF16)
    up_grad = (hidden_grad * gate_f * sig).astype(BF16)
    return mixed, combine_grad, gate_grad, up_grad, wg[None]


def solution(mesh):
    return jax.shard_map(
        per_device,
        mesh=mesh,
        in_specs=(
            P("dp", None, "hid"),
            P("dp", None, "hid"),
            P("dp", None),
            P("dp", None),
            P("dp", None),
            P("dp", "hid", None),
        ),
        out_specs=(
            P("dp", None, "hid"),
            P("dp", None),
            P("dp", None, "hid"),
            P("dp", None, "hid"),
            P("dp", "hid", None),
        ),
        check_vma=False,
    )
```

```python
import jax
import jax.numpy as jnp
from jax import lax
from jax.experimental import pallas as pl
from jax.experimental.pallas import tpu as pltpu
from jax.sharding import PartitionSpec as P

E = 8
TOP = 2
CAP = 48
F32 = jnp.float32
BF16 = jnp.bfloat16
MESH = pl.DeviceIdType.MESH


def exchange_kernel(
    hs, gs, w_hbm, oh, bh, wg, cg,
    w, hr, gr, os, orx, od, bs, br, wt, cgs, cgr,
    send_h, send_g, recv_h, recv_g, xg_send, xg_recv, sib_send, sib_recv,
    xo_send, xo_recv, bsib_send, bsib_recv, home_o_send, home_b_send,
    home_recv, wg_sem, w_sem, cg_send, cg_recv,
):
    me = lax.axis_index("dp")
    x = lax.axis_index("hid")
    z = lax.div(me, 8)
    y = lax.rem(lax.div(me, 2), 4)
    core = lax.rem(me, 2)
    e_me = lax.div(me, 4)
    j_me = lax.rem(me, 4)
    sibling = me + 1 - 2 * core
    rows_n = 8 * CAP
    q_w = gr.shape[1] // 4
    half_w = hr.shape[1] // 2

    def m(v, k):
        return pl.multiple_of(v, k)

    w_copy = pltpu.make_async_copy(w_hbm, w, w_sem)
    w_copy.start()

    barrier = pltpu.get_barrier_semaphore()

    def greet_dp(n, carry):
        peer = lax.rem(me + n, 32)
        pl.semaphore_signal(barrier, inc=1, device_id=(peer, x), device_id_type=MESH)
        return carry

    lax.fori_loop(1, 32, greet_dp, 0)
    for o in range(1, 4):
        pl.semaphore_signal(
            barrier, inc=1, device_id=(me, lax.rem(x + o, 4)), device_id_type=MESH
        )
    pl.semaphore_wait(barrier, 34)

    my_half = m(core * half_w, 128)
    other_half = m((1 - core) * half_w, 128)
    my_quarter = m(x * q_w, 128)
    my_expert_rows = m(e_me * CAP, 16)

    def base_of(r):
        return m(r * rows_n, 16)

    def partner(n, sign):
        dz = lax.rem(n, 4)
        dy = lax.rem(dz + lax.div(n, 8), 4)
        dc = lax.rem(lax.div(n, 4), 2)
        pz = lax.rem(z + sign * dz + 4, 4)
        py = lax.rem(y + sign * dy + 4, 4)
        return pz * 8 + py * 2 + lax.rem(core + dc, 2)

    def slot_rows(n, source_core):
        slot = lax.div(n, 8) * 8 + source_core * 4 + lax.rem(n, 4)
        return pl.ds(m(slot * CAP, 16), CAP)

    pltpu.make_async_copy(
        gs.at[pl.ds(my_expert_rows, CAP), pl.ds(m(j_me * q_w, 128), q_w)],
        gr.at[slot_rows(0, core), pl.ds(my_quarter, q_w)],
        recv_g.at[0],
    ).start()
    pltpu.make_async_copy(
        hs.at[pl.ds(my_expert_rows, CAP), pl.ds(my_half, half_w)],
        hr.at[slot_rows(0, core), pl.ds(my_half, half_w)],
        recv_h.at[0],
    ).start()

    def g_copy(n):
        p = partner(n, 1)
        return pltpu.make_async_remote_copy(
            src_ref=gs.at[
                pl.ds(m(lax.div(p, 4) * CAP, 16), CAP), pl.ds(m(lax.rem(p, 4) * q_w, 128), q_w)
            ],
            dst_ref=gr.at[slot_rows(n, core), pl.ds(my_quarter, q_w)],
            send_sem=send_g.at[n],
            recv_sem=recv_g.at[lax.div(n, 8)],
            device_id=(p, x),
            device_id_type=MESH,
        )

    def h_copy(n):
        p = partner(n, 1)
        cols = pl.ds(m(lax.rem(p, 2) * half_w, 128), half_w)
        return pltpu.make_async_remote_copy(
            src_ref=hs.at[pl.ds(m(lax.div(p, 4) * CAP, 16), CAP), cols],
            dst_ref=hr.at[slot_rows(n, core), cols],
            send_sem=send_h.at[n],
            recv_sem=recv_h.at[lax.div(n, 8)],
            device_id=(p, x),
            device_id_type=MESH,
        )

    def loop(lo, hi, f):
        def step(n, carry):
            f(n)
            return carry

        lax.fori_loop(lo, hi, step, 0)

    loop(1, 16, lambda n: g_copy(n).start())
    loop(1, 8, lambda n: h_copy(n).start())

    def issue(r):
        loop(r * 8, r * 8 + 8, lambda n: g_copy(n).start())
        loop(r * 8 - 8, r * 8, lambda n: h_copy(n).start())

    loop(2, 4, issue)
    loop(24, 32, lambda n: h_copy(n).start())

    def xg_copy(r, o):
        part = gr.at[pl.ds(base_of(r), rows_n), pl.ds(my_quarter, q_w)]
        return pltpu.make_async_remote_copy(
            src_ref=part, dst_ref=part,
            send_sem=xg_send.at[r, o - 1], recv_sem=xg_recv.at[r, o - 1],
            device_id=(me, lax.rem(x + o, 4)), device_id_type=MESH,
        )

    def xg_wait(r, o):
        cols = m(lax.rem(x - o + 4, 4) * q_w, 128)
        part = gr.at[pl.ds(base_of(r), rows_n), pl.ds(cols, q_w)]
        pltpu.make_async_copy(part, part, xg_recv.at[r, o - 1]).wait()

    def pass_g(r):
        part = gr.at[pl.ds(base_of(r), rows_n), pl.ds(my_quarter, q_w)]
        pltpu.make_async_copy(part, part, recv_g.at[r]).wait()
        for o in range(1, 4):
            xg_copy(r, o).start()

    def sib_copy(r):
        part = hr.at[pl.ds(base_of(r), rows_n), pl.ds(my_half, half_w)]
        return pltpu.make_async_remote_copy(
            src_ref=part, dst_ref=part, send_sem=sib_send.at[r], recv_sem=sib_recv.at[r],
            device_id=(sibling, x), device_id_type=MESH,
        )

    def pass_h(r):
        part = hr.at[pl.ds(base_of(r), rows_n), pl.ds(my_half, half_w)]
        pltpu.make_async_copy(part, part, recv_h.at[r]).wait()
        sib_copy(r).start()

    def xo_copy(r, o):
        peer = lax.rem(x + o, 4)
        return pltpu.make_async_remote_copy(
            src_ref=os.at[pl.ds(base_of(r), rows_n), pl.ds(m(peer * q_w, 128), q_w)],
            dst_ref=orx.at[o - 1, pl.ds(base_of(r), rows_n), :],
            send_sem=xo_send.at[r, o - 1], recv_sem=xo_recv.at[r, o - 1],
            device_id=(me, peer), device_id_type=MESH,
        )

    def out_product(r):
        part = hr.at[pl.ds(base_of(r), rows_n), pl.ds(other_half, half_w)]
        pltpu.make_async_copy(part, part, sib_recv.at[r]).wait()
        rows = pl.ds(base_of(r), rows_n)

        def tile(q):
            cols = pl.ds(m(q * 2 * q_w, 128), 2 * q_w)
            acc = jnp.dot(hr[rows, :], w[:, cols], preferred_element_type=F32)
            os[rows, cols] = acc.astype(BF16)

        loop(0, 2, tile)
        for o in range(1, 4):
            xo_copy(r, o).start()

    def bsib_copy(r):
        rows = pl.ds(base_of(r), rows_n)
        return pltpu.make_async_remote_copy(
            src_ref=bs.at[rows, pl.ds(other_half, half_w)],
            dst_ref=br.at[rows, :],
            send_sem=bsib_send.at[r], recv_sem=bsib_recv.at[r],
            device_id=(sibling, x), device_id_type=MESH,
        )

    def back_product(r):
        for o in range(1, 4):
            xg_wait(r, o)
        rows = pl.ds(base_of(r), rows_n)

        def tile(n):
            cols = pl.ds(m(n * 512, 128), 512)
            acc = lax.dot_general(
                gr[rows, :], w[cols, :], (((1,), (1,)), ((), ())), preferred_element_type=F32
            )
            bs[rows, cols] = acc.astype(BF16)

        loop(0, 4, tile)
        bsib_copy(r).start()

    def home_b_copy(n):
        p = partner(n, -1)
        return pltpu.make_async_remote_copy(
            src_ref=br.at[slot_rows(n, lax.rem(p, 2)), :],
            dst_ref=bh.at[
                pl.ds(m((lax.div(j_me, 2) * E + e_me) * CAP, 16), CAP), pl.ds(my_half, half_w)
            ],
            send_sem=home_b_send.at[n], recv_sem=home_recv.at[1],
            device_id=(p, x), device_id_type=MESH,
        )

    def home_o_copy(n):
        p = partner(n, -1)
        return pltpu.make_async_remote_copy(
            src_ref=od.at[slot_rows(n, lax.rem(p, 2)), :],
            dst_ref=oh.at[pl.ds(my_expert_rows, CAP), pl.ds(m(j_me * q_w, 128), q_w)],
            send_sem=home_o_send.at[n], recv_sem=home_recv.at[0],
            device_id=(p, x), device_id_type=MESH,
        )

    def back_sum(r):
        rows = pl.ds(base_of(r), rows_n)
        part = br.at[rows, :]
        pltpu.make_async_copy(part, part, bsib_recv.at[r]).wait()

        def tile(i):
            sub = pl.ds(m(base_of(r) + i * CAP, 16), CAP)
            total = br[sub, :].astype(F32) + bs[sub, pl.ds(my_half, half_w)].astype(F32)
            br[sub, :] = total.astype(BF16)

        loop(0, 8, tile)

    def out_sum(r):
        for o in range(1, 4):
            part = orx.at[o - 1, pl.ds(base_of(r), rows_n), :]
            pltpu.make_async_copy(part, part, xo_recv.at[r, o - 1]).wait()

        def tile(i):
            sub = pl.ds(m(base_of(r) + i * CAP, 16), CAP)
            total = os[sub, pl.ds(my_quarter, q_w)].astype(F32)
            for k in range(3):
                total = total + orx[k, sub, :].astype(F32)
            od[sub, :] = total.astype(BF16)

        loop(0, 8, tile)

    def wg_copy(n):
        rows = pl.ds(m(n * 256, 16), 256)
        return pltpu.make_async_copy(wt.at[rows, :], wg.at[rows, :], wg_sem.at[n])

    def wg_tile(n):
        cols = pl.ds(m(n * 256, 128), 256)
        acc = lax.dot_general(
            hr[:, cols], gr[...], (((0,), (0,)), ((), ())), preferred_element_type=F32
        )
        wt[pl.ds(m(n * 256, 16), 256), :] = acc.astype(BF16)
        wg_copy(n).start()

    def home_b(r):
        back_sum(r)

        @pl.when(r == 0)
        def _():
            pltpu.make_async_copy(
                br.at[slot_rows(0, core), :],
                bh.at[
                    pl.ds(m((lax.div(j_me, 2) * E + e_me) * CAP, 16), CAP), pl.ds(my_half, half_w)
                ],
                home_recv.at[1],
            ).start()

        loop(jnp.maximum(r * 8, 1), r * 8 + 8, lambda n: home_b_copy(n).start())

    def home_o(r):
        out_sum(r)

        @pl.when(r == 0)
        def _():
            pltpu.make_async_copy(
                od.at[slot_rows(0, core), :],
                oh.at[pl.ds(my_expert_rows, CAP), pl.ds(m(j_me * q_w, 128), q_w)],
                home_recv.at[0],
            ).start()

        loop(jnp.maximum(r * 8, 1), r * 8 + 8, lambda n: home_o_copy(n).start())

    pass_g(0)
    w_copy.wait()

    def step(r):
        @pl.when(r < 3)
        def _():
            pass_g(r + 1)

        @pl.when(r < 4)
        def _():
            pass_h(r)

        @pl.when((r > 0) & (r < 5))
        def _():
            home_b(r - 1)

        @pl.when(r > 1)
        def _():
            home_o(r - 2)

        @pl.when(r < 4)
        def _():
            out_product(r)
            back_product(r)

        @pl.when(r > 3)
        def _():
            loop(r * 4 - 16, r * 4 - 12, wg_tile)

    loop(0, 6, step)

    pltpu.make_async_copy(oh, oh, home_recv.at[0]).wait()
    fold = jnp.zeros((rows_n, 128), F32)
    for k in range(4 * q_w // 128):
        cols = slice(k * 128, (k + 1) * 128)
        fold = fold + oh[:, cols].astype(F32) * gs[:, cols].astype(F32)
    high = fold.astype(BF16)
    low = (fold - high.astype(F32)).astype(BF16)
    ones = jnp.ones((8, 128), BF16)
    last = (((1,), (1,)), ((), ()))
    cgs[...] = lax.dot_general(ones, high, last, preferred_element_type=F32) + lax.dot_general(
        ones, low, last, preferred_element_type=F32
    )

    def cg_copy(o):
        return pltpu.make_async_remote_copy(
            src_ref=cgs, dst_ref=cgr.at[o - 1],
            send_sem=cg_send.at[o - 1], recv_sem=cg_recv.at[o - 1],
            device_id=(me, lax.rem(x + o, 4)), device_id_type=MESH,
        )

    for o in range(1, 4):
        cg_copy(o).start()
    for o in range(1, 4):
        cg_copy(o).wait_recv()
    cg[...] = cgs[...] + cgr[0] + cgr[1] + cgr[2]

    pltpu.make_async_copy(bh, bh, home_recv.at[1]).wait()
    for o in range(1, 4):
        cg_copy(o).wait_send()
    loop(0, 8, lambda n: wg_copy(n).wait())

    def drain(n):
        g_copy(n).wait_send()
        h_copy(n).wait_send()
        home_b_copy(n).wait_send()
        home_o_copy(n).wait_send()

    loop(1, 32, drain)

    def drain_r(r):
        sib_copy(r).wait_send()
        bsib_copy(r).wait_send()
        for o in range(1, 4):
            xg_copy(r, o).wait_send()
            xo_copy(r, o).wait_send()

    loop(0, 4, drain_r)


def exchange(hs, gs, w):
    rows, ff = hs.shape
    width = gs.shape[1]
    rows_all = 32 * CAP
    vmem = pl.BlockSpec(memory_space=pltpu.VMEM)
    dma = pltpu.SemaphoreType.DMA
    return pl.pallas_call(
        exchange_kernel,
        out_shape=(
            jax.ShapeDtypeStruct((rows, width), BF16),
            jax.ShapeDtypeStruct((2 * rows, ff), BF16),
            jax.ShapeDtypeStruct((ff, width), BF16),
            jax.ShapeDtypeStruct((8, rows), F32),
        ),
        in_specs=[vmem, vmem, pl.BlockSpec(memory_space=pl.ANY)],
        out_specs=(vmem, vmem, pl.BlockSpec(memory_space=pl.ANY), vmem),
        scratch_shapes=[
            pltpu.VMEM((ff, width), BF16),
            pltpu.VMEM((rows_all, ff), BF16),
            pltpu.VMEM((rows_all, width), BF16),
            pltpu.VMEM((rows_all, width), BF16),
            pltpu.VMEM((3, rows_all, width // 4), BF16),
            pltpu.VMEM((rows_all, width // 4), BF16),
            pltpu.VMEM((rows_all, ff), BF16),
            pltpu.VMEM((rows_all, ff // 2), BF16),
            pltpu.VMEM((ff, width), BF16),
            pltpu.VMEM((8, rows), F32),
            pltpu.VMEM((3, 8, rows), F32),
            dma((32,)), dma((32,)), dma((4,)), dma((4,)),
            dma((4, 3)), dma((4, 3)), dma((4,)), dma((4,)),
            dma((4, 3)), dma((4, 3)), dma((4,)), dma((4,)),
            dma((32,)), dma((32,)), dma((2,)), dma((8,)), dma, dma((3,)), dma((3,)),
        ],
        compiler_params=pltpu.CompilerParams(
            collective_id=0, has_side_effects=True, vmem_limit_bytes=62 * 1024 * 1024
        ),
        cost_estimate=pl.CostEstimate(
            flops=6 * rows_all * ff * width, bytes_accessed=30000000, transcendentals=0
        ),
    )(hs, gs, w)


def per_device(gate_pre, up_pre, out_grad, combine, expert_ids, down_weight):
    tokens = gate_pre.shape[0]
    x = lax.axis_index("hid")
    width = down_weight.shape[2]
    quarter = width // 4
    rows = E * CAP
    flat = jnp.concatenate([expert_ids[:, 0], expert_ids[:, 1]])
    onehot = (flat[:, None] == jnp.arange(E, dtype=jnp.int32)[None, :]).astype(BF16)
    count = tokens * TOP
    before = (jnp.arange(count)[:, None] > jnp.arange(count)[None, :]).astype(BF16)
    earlier = jnp.dot(before, onehot, preferred_element_type=F32)
    position = jnp.sum(earlier * onehot.astype(F32), axis=1).astype(jnp.int32)
    target = flat * CAP + position
    row_ids = jnp.arange(rows, dtype=jnp.int32)
    pack = (target[None, :] == row_ids[:, None]).astype(BF16)
    hit = target[:, None] == row_ids[None, :]
    unpack = hit.astype(BF16)

    gate_f = gate_pre.astype(F32)
    up_f = up_pre.astype(F32)
    sig = jax.nn.sigmoid(gate_f)
    hidden = (gate_f * sig * up_f).astype(BF16)
    hs = (
        jnp.dot(pack[:, :tokens], hidden[:, 0], preferred_element_type=F32)
        + jnp.dot(pack[:, tokens:], hidden[:, 1], preferred_element_type=F32)
    ).astype(BF16)
    mine = jnp.concatenate(
        [
            lax.dynamic_slice_in_dim(out_grad, j * width + x * quarter, quarter, axis=1)
            for j in range(4)
        ],
        axis=1,
    ).astype(F32)
    scaled0 = (combine[:, 0:1] * mine).astype(BF16)
    scaled1 = (combine[:, 1:2] * mine).astype(BF16)
    gs = (
        jnp.dot(pack[:, :tokens], scaled0, preferred_element_type=F32)
        + jnp.dot(pack[:, tokens:], scaled1, preferred_element_type=F32)
    ).astype(BF16)

    oh, bh, wg, cg = exchange(hs, gs, down_weight[0])

    mixed = (
        combine[:, 0:1] * jnp.dot(unpack[:tokens], oh, preferred_element_type=F32)
        + combine[:, 1:2] * jnp.dot(unpack[tokens:], oh, preferred_element_type=F32)
    ).astype(BF16).reshape(tokens, 4, quarter)
    slot_cg = jnp.sum(jnp.where(hit, cg[0:1, :], 0.0), axis=1)
    combine_grad = jnp.stack([slot_cg[:tokens], slot_cg[tokens:]], axis=1) / combine
    both = jnp.concatenate([unpack, unpack], axis=1)
    hidden_grad = jnp.stack(
        [
            jnp.dot(both[:tokens], bh, preferred_element_type=F32),
            jnp.dot(both[tokens:], bh, preferred_element_type=F32),
        ],
        axis=1,
    )
    gate_grad = (hidden_grad * up_f * sig * (1.0 + gate_f * (1.0 - sig))).astype(BF16)
    up_grad = (hidden_grad * gate_f * sig).astype(BF16)
    return mixed, combine_grad, gate_grad, up_grad, wg[None]


def solution(mesh):
    return jax.shard_map(
        per_device,
        mesh=mesh,
        in_specs=(
            P("dp", None, "hid"),
            P("dp", None, "hid"),
            P("dp", None),
            P("dp", None),
            P("dp", None),
            P("dp", "hid", None),
        ),
        out_specs=(
            P("dp", None, "hid"),
            P("dp", None),
            P("dp", None, "hid"),
            P("dp", None, "hid"),
            P("dp", "hid", None),
        ),
        check_vma=False,
    )
```

```python
import jax
import jax.numpy as jnp
from jax import lax
from jax.experimental import pallas as pl
from jax.experimental.pallas import tpu as pltpu
from jax.sharding import PartitionSpec as P

E = 8
TOP = 2
CAP = 48
F32 = jnp.float32
BF16 = jnp.bfloat16
MESH = pl.DeviceIdType.MESH


def exchange_kernel(
    hs, gs, w_hbm, oh, bh, wg, cg,
    w, hr, gr, os, opx, orx, od, bs, br, wt, cgs, cgr,
    send_h, send_g, recv_h, recv_g, xg_send, xg_recv, xf_send, xf_recv, sib_send, sib_recv,
    xp_send, xp_recv, xo_send, xo_recv, bsib_send, bsib_recv, home_o_send, home_b_send,
    home_recv, wg_sem, w_sem, cg_send, cg_recv,
):
    me = lax.axis_index("dp")
    x = lax.axis_index("hid")
    z = lax.div(me, 8)
    y = lax.rem(lax.div(me, 2), 4)
    core = lax.rem(me, 2)
    e_me = lax.div(me, 4)
    j_me = lax.rem(me, 4)
    sibling = me + 1 - 2 * core
    rows_n = 8 * CAP
    q_w = gr.shape[1] // 4
    half_w = hr.shape[1] // 2

    def m(v, k):
        return pl.multiple_of(v, k)

    w_copy = pltpu.make_async_copy(w_hbm, w, w_sem)
    w_copy.start()

    barrier = pltpu.get_barrier_semaphore()

    def greet_dp(n, carry):
        peer = lax.rem(me + n, 32)
        pl.semaphore_signal(barrier, inc=1, device_id=(peer, x), device_id_type=MESH)
        return carry

    lax.fori_loop(1, 32, greet_dp, 0)
    for o in range(1, 4):
        pl.semaphore_signal(
            barrier, inc=1, device_id=(me, lax.rem(x + o, 4)), device_id_type=MESH
        )
    pl.semaphore_wait(barrier, 34)

    my_half = m(core * half_w, 128)
    other_half = m((1 - core) * half_w, 128)
    my_quarter = m(x * q_w, 128)
    my_expert_rows = m(e_me * CAP, 16)

    def base_of(r):
        return m(r * rows_n, 16)

    def partner(n, sign):
        dz = lax.rem(n, 4)
        dy = lax.rem(dz + lax.div(n, 8), 4)
        dc = lax.rem(lax.div(n, 4), 2)
        pz = lax.rem(z + sign * dz + 4, 4)
        py = lax.rem(y + sign * dy + 4, 4)
        return pz * 8 + py * 2 + lax.rem(core + dc, 2)

    def slot_rows(n, source_core):
        slot = lax.div(n, 8) * 8 + source_core * 4 + lax.rem(n, 4)
        return pl.ds(m(slot * CAP, 16), CAP)

    pltpu.make_async_copy(
        gs.at[pl.ds(my_expert_rows, CAP), pl.ds(m(j_me * q_w, 128), q_w)],
        gr.at[slot_rows(0, core), pl.ds(my_quarter, q_w)],
        recv_g.at[0],
    ).start()
    pltpu.make_async_copy(
        hs.at[pl.ds(my_expert_rows, CAP), pl.ds(my_half, half_w)],
        hr.at[slot_rows(0, core), pl.ds(my_half, half_w)],
        recv_h.at[0],
    ).start()

    def g_copy(n):
        p = partner(n, 1)
        return pltpu.make_async_remote_copy(
            src_ref=gs.at[
                pl.ds(m(lax.div(p, 4) * CAP, 16), CAP), pl.ds(m(lax.rem(p, 4) * q_w, 128), q_w)
            ],
            dst_ref=gr.at[slot_rows(n, core), pl.ds(my_quarter, q_w)],
            send_sem=send_g.at[n],
            recv_sem=recv_g.at[lax.div(n, 8)],
            device_id=(p, x),
            device_id_type=MESH,
        )

    def h_copy(n):
        p = partner(n, 1)
        cols = pl.ds(m(lax.rem(p, 2) * half_w, 128), half_w)
        return pltpu.make_async_remote_copy(
            src_ref=hs.at[pl.ds(m(lax.div(p, 4) * CAP, 16), CAP), cols],
            dst_ref=hr.at[slot_rows(n, core), cols],
            send_sem=send_h.at[n],
            recv_sem=recv_h.at[lax.div(n, 8)],
            device_id=(p, x),
            device_id_type=MESH,
        )

    def loop(lo, hi, f):
        def step(n, carry):
            f(n)
            return carry

        lax.fori_loop(lo, hi, step, 0)

    loop(1, 16, lambda n: g_copy(n).start())
    loop(1, 8, lambda n: h_copy(n).start())

    def issue(r):
        loop(r * 8, r * 8 + 8, lambda n: g_copy(n).start())
        loop(r * 8 - 8, r * 8, lambda n: h_copy(n).start())

    loop(2, 4, issue)
    loop(24, 32, lambda n: h_copy(n).start())

    half_rows = rows_n // 2

    def neighbour(d):
        return lax.rem(x + (1, 3)[d], 4)

    def quarter_at(offset):
        return pl.ds(m(lax.rem(x + offset, 4) * q_w, 128), q_w)

    def half_of(r, d):
        return pl.ds(m(r * rows_n + d * half_rows, 16), half_rows)

    def xg_copy(r, d):
        part = gr.at[pl.ds(base_of(r), rows_n), quarter_at(0)]
        return pltpu.make_async_remote_copy(
            src_ref=part, dst_ref=part,
            send_sem=xg_send.at[r, d], recv_sem=xg_recv.at[r, d],
            device_id=(me, neighbour(d)), device_id_type=MESH,
        )

    def xf_copy(r, d):
        part = gr.at[half_of(r, d), quarter_at((3, 1)[d])]
        return pltpu.make_async_remote_copy(
            src_ref=part, dst_ref=part,
            send_sem=xf_send.at[r, d], recv_sem=xf_recv.at[r, d],
            device_id=(me, neighbour(d)), device_id_type=MESH,
        )

    def pass_g(r):
        part = gr.at[pl.ds(base_of(r), rows_n), quarter_at(0)]
        pltpu.make_async_copy(part, part, recv_g.at[r]).wait()
        for d in range(2):
            xg_copy(r, d).start()

    def forward_g(r):
        for d in range(2):
            part = gr.at[pl.ds(base_of(r), rows_n), quarter_at((3, 1)[d])]
            pltpu.make_async_copy(part, part, xg_recv.at[r, d]).wait()
            xf_copy(r, d).start()

    def sib_copy(r):
        part = hr.at[pl.ds(base_of(r), rows_n), pl.ds(my_half, half_w)]
        return pltpu.make_async_remote_copy(
            src_ref=part, dst_ref=part, send_sem=sib_send.at[r], recv_sem=sib_recv.at[r],
            device_id=(sibling, x), device_id_type=MESH,
        )

    def pass_h(r):
        part = hr.at[pl.ds(base_of(r), rows_n), pl.ds(my_half, half_w)]
        pltpu.make_async_copy(part, part, recv_h.at[r]).wait()
        sib_copy(r).start()

    def xp_copy(r, d):
        return pltpu.make_async_remote_copy(
            src_ref=os.at[half_of(r, d), quarter_at(2)],
            dst_ref=opx.at[d, pl.ds(m(r * half_rows, 16), half_rows), :],
            send_sem=xp_send.at[r, d], recv_sem=xp_recv.at[r, d],
            device_id=(me, neighbour(d)), device_id_type=MESH,
        )

    def xo_copy(r, d):
        return pltpu.make_async_remote_copy(
            src_ref=os.at[pl.ds(base_of(r), rows_n), quarter_at((1, 3)[d])],
            dst_ref=orx.at[d, pl.ds(base_of(r), rows_n), :],
            send_sem=xo_send.at[r, d], recv_sem=xo_recv.at[r, d],
            device_id=(me, neighbour(d)), device_id_type=MESH,
        )

    def pass_out(r):
        for d in range(2):
            part = opx.at[d, pl.ds(m(r * half_rows, 16), half_rows), :]
            pltpu.make_async_copy(part, part, xp_recv.at[r, d]).wait()

            def tile(i):
                sub = pl.ds(m(r * rows_n + d * half_rows + i * CAP, 16), CAP)
                come = opx[d, pl.ds(m(r * half_rows + i * CAP, 16), CAP), :]
                cols = quarter_at((1, 3)[d])
                os[sub, cols] = (os[sub, cols].astype(F32) + come.astype(F32)).astype(BF16)

            loop(0, half_rows // CAP, tile)
            xo_copy(r, d).start()

    def out_product(r):
        part = hr.at[pl.ds(base_of(r), rows_n), pl.ds(other_half, half_w)]
        pltpu.make_async_copy(part, part, sib_recv.at[r]).wait()
        rows = pl.ds(base_of(r), rows_n)

        def tile(q):
            cols = pl.ds(m(q * 2 * q_w, 128), 2 * q_w)
            acc = jnp.dot(hr[rows, :], w[:, cols], preferred_element_type=F32)
            os[rows, cols] = acc.astype(BF16)

        loop(0, 2, tile)
        for d in range(2):
            xp_copy(r, d).start()

    def bsib_copy(r):
        rows = pl.ds(base_of(r), rows_n)
        return pltpu.make_async_remote_copy(
            src_ref=bs.at[rows, pl.ds(other_half, half_w)],
            dst_ref=br.at[rows, :],
            send_sem=bsib_send.at[r], recv_sem=bsib_recv.at[r],
            device_id=(sibling, x), device_id_type=MESH,
        )

    def back_product(r):
        for d in range(2):
            part = gr.at[half_of(r, d), quarter_at(2)]
            pltpu.make_async_copy(part, part, xf_recv.at[r, d]).wait()
        rows = pl.ds(base_of(r), rows_n)

        def tile(n):
            cols = pl.ds(m(n * 512, 128), 512)
            acc = lax.dot_general(
                gr[rows, :], w[cols, :], (((1,), (1,)), ((), ())), preferred_element_type=F32
            )
            bs[rows, cols] = acc.astype(BF16)

        loop(0, 4, tile)
        bsib_copy(r).start()

    def home_b_copy(n):
        p = partner(n, -1)
        return pltpu.make_async_remote_copy(
            src_ref=br.at[slot_rows(n, lax.rem(p, 2)), :],
            dst_ref=bh.at[
                pl.ds(m((lax.div(j_me, 2) * E + e_me) * CAP, 16), CAP), pl.ds(my_half, half_w)
            ],
            send_sem=home_b_send.at[n], recv_sem=home_recv.at[1],
            device_id=(p, x), device_id_type=MESH,
        )

    def home_o_copy(n):
        p = partner(n, -1)
        return pltpu.make_async_remote_copy(
            src_ref=od.at[slot_rows(n, lax.rem(p, 2)), :],
            dst_ref=oh.at[pl.ds(my_expert_rows, CAP), pl.ds(m(j_me * q_w, 128), q_w)],
            send_sem=home_o_send.at[n], recv_sem=home_recv.at[0],
            device_id=(p, x), device_id_type=MESH,
        )

    def back_sum(r):
        rows = pl.ds(base_of(r), rows_n)
        part = br.at[rows, :]
        pltpu.make_async_copy(part, part, bsib_recv.at[r]).wait()

        def tile(i):
            sub = pl.ds(m(base_of(r) + i * CAP, 16), CAP)
            total = br[sub, :].astype(F32) + bs[sub, pl.ds(my_half, half_w)].astype(F32)
            br[sub, :] = total.astype(BF16)

        loop(0, 8, tile)

    def out_sum(r):
        for d in range(2):
            part = orx.at[d, pl.ds(base_of(r), rows_n), :]
            pltpu.make_async_copy(part, part, xo_recv.at[r, d]).wait()

        def tile(i):
            sub = pl.ds(m(base_of(r) + i * CAP, 16), CAP)
            total = os[sub, pl.ds(my_quarter, q_w)].astype(F32)
            for k in range(2):
                total = total + orx[k, sub, :].astype(F32)
            od[sub, :] = total.astype(BF16)

        loop(0, 8, tile)

    def wg_copy(n):
        rows = pl.ds(m(n * 256, 16), 256)
        return pltpu.make_async_copy(wt.at[rows, :], wg.at[rows, :], wg_sem.at[n])

    def wg_tile(n):
        cols = pl.ds(m(n * 256, 128), 256)
        acc = lax.dot_general(
            hr[:, cols], gr[...], (((0,), (0,)), ((), ())), preferred_element_type=F32
        )
        wt[pl.ds(m(n * 256, 16), 256), :] = acc.astype(BF16)
        wg_copy(n).start()

    def home_b(r):
        back_sum(r)

        @pl.when(r == 0)
        def _():
            pltpu.make_async_copy(
                br.at[slot_rows(0, core), :],
                bh.at[
                    pl.ds(m((lax.div(j_me, 2) * E + e_me) * CAP, 16), CAP), pl.ds(my_half, half_w)
                ],
                home_recv.at[1],
            ).start()

        loop(jnp.maximum(r * 8, 1), r * 8 + 8, lambda n: home_b_copy(n).start())

    def home_o(r):
        out_sum(r)

        @pl.when(r == 0)
        def _():
            pltpu.make_async_copy(
                od.at[slot_rows(0, core), :],
                oh.at[pl.ds(my_expert_rows, CAP), pl.ds(m(j_me * q_w, 128), q_w)],
                home_recv.at[0],
            ).start()

        loop(jnp.maximum(r * 8, 1), r * 8 + 8, lambda n: home_o_copy(n).start())

    pass_g(0)
    pass_g(1)
    forward_g(0)
    w_copy.wait()

    def step(r):
        @pl.when(r < 2)
        def _():
            pass_g(r + 2)

        @pl.when(r < 3)
        def _():
            forward_g(r + 1)

        @pl.when(r < 4)
        def _():
            pass_h(r)

        @pl.when((r > 0) & (r < 5))
        def _():
            home_b(r - 1)

        @pl.when(r > 1)
        def _():
            home_o(r - 2)

        @pl.when(r < 4)
        def _():
            out_product(r)
            back_product(r)
            pass_out(r)

        @pl.when(r > 3)
        def _():
            loop(r * 4 - 16, r * 4 - 12, wg_tile)

    loop(0, 6, step)

    pltpu.make_async_copy(oh, oh, home_recv.at[0]).wait()
    fold = jnp.zeros((rows_n, 128), F32)
    for k in range(4 * q_w // 128):
        cols = slice(k * 128, (k + 1) * 128)
        fold = fold + oh[:, cols].astype(F32) * gs[:, cols].astype(F32)
    high = fold.astype(BF16)
    low = (fold - high.astype(F32)).astype(BF16)
    ones = jnp.ones((8, 128), BF16)
    last = (((1,), (1,)), ((), ()))
    cgs[...] = lax.dot_general(ones, high, last, preferred_element_type=F32) + lax.dot_general(
        ones, low, last, preferred_element_type=F32
    )

    def cg_copy(o):
        return pltpu.make_async_remote_copy(
            src_ref=cgs, dst_ref=cgr.at[o - 1],
            send_sem=cg_send.at[o - 1], recv_sem=cg_recv.at[o - 1],
            device_id=(me, lax.rem(x + o, 4)), device_id_type=MESH,
        )

    for o in range(1, 4):
        cg_copy(o).start()
    for o in range(1, 4):
        cg_copy(o).wait_recv()
    cg[...] = cgs[...] + cgr[0] + cgr[1] + cgr[2]

    pltpu.make_async_copy(bh, bh, home_recv.at[1]).wait()
    for o in range(1, 4):
        cg_copy(o).wait_send()
    loop(0, 8, lambda n: wg_copy(n).wait())

    def drain(n):
        g_copy(n).wait_send()
        h_copy(n).wait_send()
        home_b_copy(n).wait_send()
        home_o_copy(n).wait_send()

    loop(1, 32, drain)

    def drain_r(r):
        sib_copy(r).wait_send()
        bsib_copy(r).wait_send()
        for d in range(2):
            xg_copy(r, d).wait_send()
            xf_copy(r, d).wait_send()
            xp_copy(r, d).wait_send()
            xo_copy(r, d).wait_send()

    loop(0, 4, drain_r)


def exchange(hs, gs, w):
    rows, ff = hs.shape
    width = gs.shape[1]
    rows_all = 32 * CAP
    vmem = pl.BlockSpec(memory_space=pltpu.VMEM)
    dma = pltpu.SemaphoreType.DMA
    return pl.pallas_call(
        exchange_kernel,
        out_shape=(
            jax.ShapeDtypeStruct((rows, width), BF16),
            jax.ShapeDtypeStruct((2 * rows, ff), BF16),
            jax.ShapeDtypeStruct((ff, width), BF16),
            jax.ShapeDtypeStruct((8, rows), F32),
        ),
        in_specs=[vmem, vmem, pl.BlockSpec(memory_space=pl.ANY)],
        out_specs=(vmem, vmem, pl.BlockSpec(memory_space=pl.ANY), vmem),
        scratch_shapes=[
            pltpu.VMEM((ff, width), BF16),
            pltpu.VMEM((rows_all, ff), BF16),
            pltpu.VMEM((rows_all, width), BF16),
            pltpu.VMEM((rows_all, width), BF16),
            pltpu.VMEM((2, rows_all // 2, width // 4), BF16),
            pltpu.VMEM((2, rows_all, width // 4), BF16),
            pltpu.VMEM((rows_all, width // 4), BF16),
            pltpu.VMEM((rows_all, ff), BF16),
            pltpu.VMEM((rows_all, ff // 2), BF16),
            pltpu.VMEM((ff, width), BF16),
            pltpu.VMEM((8, rows), F32),
            pltpu.VMEM((3, 8, rows), F32),
            dma((32,)), dma((32,)), dma((4,)), dma((4,)),
            dma((4, 2)), dma((4, 2)), dma((4, 2)), dma((4, 2)), dma((4,)), dma((4,)),
            dma((4, 2)), dma((4, 2)), dma((4, 2)), dma((4, 2)), dma((4,)), dma((4,)),
            dma((32,)), dma((32,)), dma((2,)), dma((8,)), dma, dma((3,)), dma((3,)),
        ],
        compiler_params=pltpu.CompilerParams(
            collective_id=0, has_side_effects=True, vmem_limit_bytes=62 * 1024 * 1024
        ),
        cost_estimate=pl.CostEstimate(
            flops=6 * rows_all * ff * width, bytes_accessed=30000000, transcendentals=0
        ),
    )(hs, gs, w)


def per_device(gate_pre, up_pre, out_grad, combine, expert_ids, down_weight):
    tokens = gate_pre.shape[0]
    x = lax.axis_index("hid")
    width = down_weight.shape[2]
    quarter = width // 4
    rows = E * CAP
    flat = jnp.concatenate([expert_ids[:, 0], expert_ids[:, 1]])
    onehot = (flat[:, None] == jnp.arange(E, dtype=jnp.int32)[None, :]).astype(BF16)
    count = tokens * TOP
    before = (jnp.arange(count)[:, None] > jnp.arange(count)[None, :]).astype(BF16)
    earlier = jnp.dot(before, onehot, preferred_element_type=F32)
    position = jnp.sum(earlier * onehot.astype(F32), axis=1).astype(jnp.int32)
    target = flat * CAP + position
    row_ids = jnp.arange(rows, dtype=jnp.int32)
    pack = (target[None, :] == row_ids[:, None]).astype(BF16)
    hit = target[:, None] == row_ids[None, :]
    unpack = hit.astype(BF16)

    gate_f = gate_pre.astype(F32)
    up_f = up_pre.astype(F32)
    sig = jax.nn.sigmoid(gate_f)
    hidden = (gate_f * sig * up_f).astype(BF16)
    hs = (
        jnp.dot(pack[:, :tokens], hidden[:, 0], preferred_element_type=F32)
        + jnp.dot(pack[:, tokens:], hidden[:, 1], preferred_element_type=F32)
    ).astype(BF16)
    mine = jnp.concatenate(
        [
            lax.dynamic_slice_in_dim(out_grad, j * width + x * quarter, quarter, axis=1)
            for j in range(4)
        ],
        axis=1,
    ).astype(F32)
    scaled0 = (combine[:, 0:1] * mine).astype(BF16)
    scaled1 = (combine[:, 1:2] * mine).astype(BF16)
    gs = (
        jnp.dot(pack[:, :tokens], scaled0, preferred_element_type=F32)
        + jnp.dot(pack[:, tokens:], scaled1, preferred_element_type=F32)
    ).astype(BF16)

    oh, bh, wg, cg = exchange(hs, gs, down_weight[0])

    mixed = (
        combine[:, 0:1] * jnp.dot(unpack[:tokens], oh, preferred_element_type=F32)
        + combine[:, 1:2] * jnp.dot(unpack[tokens:], oh, preferred_element_type=F32)
    ).astype(BF16).reshape(tokens, 4, quarter)
    slot_cg = jnp.sum(jnp.where(hit, cg[0:1, :], 0.0), axis=1)
    combine_grad = jnp.stack([slot_cg[:tokens], slot_cg[tokens:]], axis=1) / combine
    both = jnp.concatenate([unpack, unpack], axis=1)
    hidden_grad = jnp.stack(
        [
            jnp.dot(both[:tokens], bh, preferred_element_type=F32),
            jnp.dot(both[tokens:], bh, preferred_element_type=F32),
        ],
        axis=1,
    )
    gate_grad = (hidden_grad * up_f * sig * (1.0 + gate_f * (1.0 - sig))).astype(BF16)
    up_grad = (hidden_grad * gate_f * sig).astype(BF16)
    return mixed, combine_grad, gate_grad, up_grad, wg[None]


def solution(mesh):
    return jax.shard_map(
        per_device,
        mesh=mesh,
        in_specs=(
            P("dp", None, "hid"),
            P("dp", None, "hid"),
            P("dp", None),
            P("dp", None),
            P("dp", None),
            P("dp", "hid", None),
        ),
        out_specs=(
            P("dp", None, "hid"),
            P("dp", None),
            P("dp", None, "hid"),
            P("dp", None, "hid"),
            P("dp", "hid", None),
        ),
        check_vma=False,
    )
```

```python
import jax
import jax.numpy as jnp
from jax import lax
from jax.experimental import pallas as pl
from jax.experimental.pallas import tpu as pltpu
from jax.sharding import PartitionSpec as P

E = 8
TOP = 2
CAP = 48
F32 = jnp.float32
BF16 = jnp.bfloat16
MESH = pl.DeviceIdType.MESH


def exchange_kernel(
    pack, unpack, h0, h1, comb, grad_hbm, w_hbm, mixed, hg, wg, cg,
    mine, hs, gs, oh, bh, w, hr, gr, os, opx, orx, od, bs, br, wt, cgs, cgr,
    send_h, send_g, recv_h, recv_g, xg_send, xg_recv, xf_send, xf_recv, sib_send, sib_recv,
    xp_send, xp_recv, xo_send, xo_recv, bsib_send, bsib_recv, home_o_send, home_b_send,
    home_recv, wg_sem, w_sem, mine_sem, cg_send, cg_recv,
):
    me = lax.axis_index("dp")
    x = lax.axis_index("hid")
    z = lax.div(me, 8)
    y = lax.rem(lax.div(me, 2), 4)
    core = lax.rem(me, 2)
    e_me = lax.div(me, 4)
    j_me = lax.rem(me, 4)
    sibling = me + 1 - 2 * core
    rows_n = 8 * CAP
    q_w = gr.shape[1] // 4
    half_w = hr.shape[1] // 2

    def m(v, k):
        return pl.multiple_of(v, k)

    def mine_copy(j):
        cols = pl.ds(m(j * 4 * q_w + x * q_w, 128), q_w)
        return pltpu.make_async_copy(
            grad_hbm.at[:, cols], mine.at[:, j * q_w : (j + 1) * q_w], mine_sem.at[j]
        )

    for j in range(4):
        mine_copy(j).start()
    w_copy = pltpu.make_async_copy(w_hbm, w, w_sem)
    w_copy.start()

    barrier = pltpu.get_barrier_semaphore()

    def greet_dp(n, carry):
        peer = lax.rem(me + n, 32)
        pl.semaphore_signal(barrier, inc=1, device_id=(peer, x), device_id_type=MESH)
        return carry

    lax.fori_loop(1, 32, greet_dp, 0)
    for o in range(1, 4):
        pl.semaphore_signal(
            barrier, inc=1, device_id=(me, lax.rem(x + o, 4)), device_id_type=MESH
        )

    tokens = mine.shape[0]
    for j in range(4):
        mine_copy(j).wait()
        cols = slice(j * q_w, (j + 1) * q_w)
        part = mine[:, cols].astype(F32)
        rows = jnp.dot(
            pack[:, :tokens], (comb[:, 0:1] * part).astype(BF16), preferred_element_type=F32
        ) + jnp.dot(
            pack[:, tokens:], (comb[:, 1:2] * part).astype(BF16), preferred_element_type=F32
        )
        gs[:, cols] = rows.astype(BF16)
    pl.semaphore_wait(barrier, 34)

    my_half = m(core * half_w, 128)
    other_half = m((1 - core) * half_w, 128)
    my_quarter = m(x * q_w, 128)
    my_expert_rows = m(e_me * CAP, 16)

    def base_of(r):
        return m(r * rows_n, 16)

    def partner(n, sign):
        dz = lax.rem(n, 4)
        dy = lax.rem(dz + lax.div(n, 8), 4)
        dc = lax.rem(lax.div(n, 4), 2)
        pz = lax.rem(z + sign * dz + 4, 4)
        py = lax.rem(y + sign * dy + 4, 4)
        return pz * 8 + py * 2 + lax.rem(core + dc, 2)

    def slot_rows(n, source_core):
        slot = lax.div(n, 8) * 8 + source_core * 4 + lax.rem(n, 4)
        return pl.ds(m(slot * CAP, 16), CAP)

    pltpu.make_async_copy(
        gs.at[pl.ds(my_expert_rows, CAP), pl.ds(m(j_me * q_w, 128), q_w)],
        gr.at[slot_rows(0, core), pl.ds(my_quarter, q_w)],
        recv_g.at[0],
    ).start()

    def g_copy(n):
        p = partner(n, 1)
        return pltpu.make_async_remote_copy(
            src_ref=gs.at[
                pl.ds(m(lax.div(p, 4) * CAP, 16), CAP), pl.ds(m(lax.rem(p, 4) * q_w, 128), q_w)
            ],
            dst_ref=gr.at[slot_rows(n, core), pl.ds(my_quarter, q_w)],
            send_sem=send_g.at[n],
            recv_sem=recv_g.at[lax.div(n, 8)],
            device_id=(p, x),
            device_id_type=MESH,
        )

    def h_copy(n):
        p = partner(n, 1)
        cols = pl.ds(m(lax.rem(p, 2) * half_w, 128), half_w)
        return pltpu.make_async_remote_copy(
            src_ref=hs.at[pl.ds(m(lax.div(p, 4) * CAP, 16), CAP), cols],
            dst_ref=hr.at[slot_rows(n, core), cols],
            send_sem=send_h.at[n],
            recv_sem=recv_h.at[lax.div(n, 8)],
            device_id=(p, x),
            device_id_type=MESH,
        )

    def loop(lo, hi, f):
        def step(n, carry):
            f(n)
            return carry

        lax.fori_loop(lo, hi, step, 0)

    loop(1, 32, lambda n: g_copy(n).start())

    def pack_h(n):
        cols = pl.ds(m(n * 512, 128), 512)
        rows = jnp.dot(pack[:, :tokens], h0[:, cols], preferred_element_type=F32) + jnp.dot(
            pack[:, tokens:], h1[:, cols], preferred_element_type=F32
        )
        hs[:, cols] = rows.astype(BF16)

    loop(0, hr.shape[1] // 512, pack_h)
    pltpu.make_async_copy(
        hs.at[pl.ds(my_expert_rows, CAP), pl.ds(my_half, half_w)],
        hr.at[slot_rows(0, core), pl.ds(my_half, half_w)],
        recv_h.at[0],
    ).start()
    loop(1, 32, lambda n: h_copy(n).start())

    half_rows = rows_n // 2

    def neighbour(d):
        return lax.rem(x + (1, 3)[d], 4)

    def quarter_at(offset):
        return pl.ds(m(lax.rem(x + offset, 4) * q_w, 128), q_w)

    def half_of(r, d):
        return pl.ds(m(r * rows_n + d * half_rows, 16), half_rows)

    def xg_copy(r, d):
        part = gr.at[pl.ds(base_of(r), rows_n), quarter_at(0)]
        return pltpu.make_async_remote_copy(
            src_ref=part, dst_ref=part,
            send_sem=xg_send.at[r, d], recv_sem=xg_recv.at[r, d],
            device_id=(me, neighbour(d)), device_id_type=MESH,
        )

    def xf_copy(r, d):
        part = gr.at[half_of(r, d), quarter_at((3, 1)[d])]
        return pltpu.make_async_remote_copy(
            src_ref=part, dst_ref=part,
            send_sem=xf_send.at[r, d], recv_sem=xf_recv.at[r, d],
            device_id=(me, neighbour(d)), device_id_type=MESH,
        )

    def pass_g(r):
        part = gr.at[pl.ds(base_of(r), rows_n), quarter_at(0)]
        pltpu.make_async_copy(part, part, recv_g.at[r]).wait()
        for d in range(2):
            xg_copy(r, d).start()

    def forward_g(r):
        for d in range(2):
            part = gr.at[pl.ds(base_of(r), rows_n), quarter_at((3, 1)[d])]
            pltpu.make_async_copy(part, part, xg_recv.at[r, d]).wait()
            xf_copy(r, d).start()

    def sib_copy(r):
        part = hr.at[pl.ds(base_of(r), rows_n), pl.ds(my_half, half_w)]
        return pltpu.make_async_remote_copy(
            src_ref=part, dst_ref=part, send_sem=sib_send.at[r], recv_sem=sib_recv.at[r],
            device_id=(sibling, x), device_id_type=MESH,
        )

    def pass_h(r):
        part = hr.at[pl.ds(base_of(r), rows_n), pl.ds(my_half, half_w)]
        pltpu.make_async_copy(part, part, recv_h.at[r]).wait()
        sib_copy(r).start()

    def xp_copy(r, d):
        return pltpu.make_async_remote_copy(
            src_ref=os.at[half_of(r, d), quarter_at(2)],
            dst_ref=opx.at[d, pl.ds(m(r * half_rows, 16), half_rows), :],
            send_sem=xp_send.at[r, d], recv_sem=xp_recv.at[r, d],
            device_id=(me, neighbour(d)), device_id_type=MESH,
        )

    def xo_copy(r, d):
        return pltpu.make_async_remote_copy(
            src_ref=os.at[pl.ds(base_of(r), rows_n), quarter_at((1, 3)[d])],
            dst_ref=orx.at[d, pl.ds(base_of(r), rows_n), :],
            send_sem=xo_send.at[r, d], recv_sem=xo_recv.at[r, d],
            device_id=(me, neighbour(d)), device_id_type=MESH,
        )

    def pass_out(r):
        for d in range(2):
            part = opx.at[d, pl.ds(m(r * half_rows, 16), half_rows), :]
            pltpu.make_async_copy(part, part, xp_recv.at[r, d]).wait()

            def tile(i):
                sub = pl.ds(m(r * rows_n + d * half_rows + i * CAP, 16), CAP)
                come = opx[d, pl.ds(m(r * half_rows + i * CAP, 16), CAP), :]
                cols = quarter_at((1, 3)[d])
                os[sub, cols] = (os[sub, cols].astype(F32) + come.astype(F32)).astype(BF16)

            loop(0, half_rows // CAP, tile)
            xo_copy(r, d).start()

    def out_product(r):
        part = hr.at[pl.ds(base_of(r), rows_n), pl.ds(other_half, half_w)]
        pltpu.make_async_copy(part, part, sib_recv.at[r]).wait()
        rows = pl.ds(base_of(r), rows_n)

        def tile(q):
            cols = pl.ds(m(q * 2 * q_w, 128), 2 * q_w)
            acc = jnp.dot(hr[rows, :], w[:, cols], preferred_element_type=F32)
            os[rows, cols] = acc.astype(BF16)

        loop(0, 2, tile)
        for d in range(2):
            xp_copy(r, d).start()

    def bsib_copy(r):
        rows = pl.ds(base_of(r), rows_n)
        return pltpu.make_async_remote_copy(
            src_ref=bs.at[rows, pl.ds(other_half, half_w)],
            dst_ref=br.at[rows, :],
            send_sem=bsib_send.at[r], recv_sem=bsib_recv.at[r],
            device_id=(sibling, x), device_id_type=MESH,
        )

    def back_product(r):
        for d in range(2):
            part = gr.at[half_of(r, d), quarter_at(2)]
            pltpu.make_async_copy(part, part, xf_recv.at[r, d]).wait()
        rows = pl.ds(base_of(r), rows_n)

        def tile(n):
            cols = pl.ds(m(n * 512, 128), 512)
            acc = lax.dot_general(
                gr[rows, :], w[cols, :], (((1,), (1,)), ((), ())), preferred_element_type=F32
            )
            bs[rows, cols] = acc.astype(BF16)

        loop(0, 4, tile)
        bsib_copy(r).start()

    def home_b_copy(n):
        p = partner(n, -1)
        return pltpu.make_async_remote_copy(
            src_ref=br.at[slot_rows(n, lax.rem(p, 2)), :],
            dst_ref=bh.at[
                pl.ds(m((lax.div(j_me, 2) * E + e_me) * CAP, 16), CAP), pl.ds(my_half, half_w)
            ],
            send_sem=home_b_send.at[n], recv_sem=home_recv.at[1],
            device_id=(p, x), device_id_type=MESH,
        )

    def home_o_copy(n):
        p = partner(n, -1)
        return pltpu.make_async_remote_copy(
            src_ref=od.at[slot_rows(n, lax.rem(p, 2)), :],
            dst_ref=oh.at[pl.ds(my_expert_rows, CAP), pl.ds(m(j_me * q_w, 128), q_w)],
            send_sem=home_o_send.at[n], recv_sem=home_recv.at[0],
            device_id=(p, x), device_id_type=MESH,
        )

    def back_sum(r):
        rows = pl.ds(base_of(r), rows_n)
        part = br.at[rows, :]
        pltpu.make_async_copy(part, part, bsib_recv.at[r]).wait()

        def tile(i):
            sub = pl.ds(m(base_of(r) + i * CAP, 16), CAP)
            total = br[sub, :].astype(F32) + bs[sub, pl.ds(my_half, half_w)].astype(F32)
            br[sub, :] = total.astype(BF16)

        loop(0, 8, tile)

    def out_sum(r):
        for d in range(2):
            part = orx.at[d, pl.ds(base_of(r), rows_n), :]
            pltpu.make_async_copy(part, part, xo_recv.at[r, d]).wait()

        def tile(i):
            sub = pl.ds(m(base_of(r) + i * CAP, 16), CAP)
            total = os[sub, pl.ds(my_quarter, q_w)].astype(F32)
            for k in range(2):
                total = total + orx[k, sub, :].astype(F32)
            od[sub, :] = total.astype(BF16)

        loop(0, 8, tile)

    def wg_copy(n):
        rows = pl.ds(m(n * 256, 16), 256)
        return pltpu.make_async_copy(wt.at[rows, :], wg.at[rows, :], wg_sem.at[n])

    def wg_tile(n):
        cols = pl.ds(m(n * 256, 128), 256)
        acc = lax.dot_general(
            hr[:, cols], gr[...], (((0,), (0,)), ((), ())), preferred_element_type=F32
        )
        wt[pl.ds(m(n * 256, 16), 256), :] = acc.astype(BF16)
        wg_copy(n).start()

    def home_b(r):
        back_sum(r)

        @pl.when(r == 0)
        def _():
            pltpu.make_async_copy(
                br.at[slot_rows(0, core), :],
                bh.at[
                    pl.ds(m((lax.div(j_me, 2) * E + e_me) * CAP, 16), CAP), pl.ds(my_half, half_w)
                ],
                home_recv.at[1],
            ).start()

        loop(jnp.maximum(r * 8, 1), r * 8 + 8, lambda n: home_b_copy(n).start())

    def home_o(r):
        out_sum(r)

        @pl.when(r == 0)
        def _():
            pltpu.make_async_copy(
                od.at[slot_rows(0, core), :],
                oh.at[pl.ds(my_expert_rows, CAP), pl.ds(m(j_me * q_w, 128), q_w)],
                home_recv.at[0],
            ).start()

        loop(jnp.maximum(r * 8, 1), r * 8 + 8, lambda n: home_o_copy(n).start())

    pass_g(0)
    pass_g(1)
    forward_g(0)
    w_copy.wait()

    def step(r):
        @pl.when(r < 2)
        def _():
            pass_g(r + 2)

        @pl.when(r < 3)
        def _():
            forward_g(r + 1)

        @pl.when(r < 4)
        def _():
            pass_h(r)

        @pl.when((r > 0) & (r < 5))
        def _():
            home_b(r - 1)

        @pl.when(r > 1)
        def _():
            home_o(r - 2)

        @pl.when(r < 4)
        def _():
            out_product(r)
            back_product(r)
            pass_out(r)

        @pl.when(r > 3)
        def _():
            loop(r * 4 - 16, r * 4 - 12, wg_tile)

    loop(0, 6, step)

    pltpu.make_async_copy(oh, oh, home_recv.at[0]).wait()
    ones = jnp.ones((8, 128), BF16)
    last = (((1,), (1,)), ((), ()))
    folds = [jnp.zeros((tokens, 128), F32), jnp.zeros((tokens, 128), F32)]
    for j in range(4):
        cols = slice(j * q_w, (j + 1) * q_w)
        part = mine[:, cols].astype(F32)
        total = None
        for t in range(2):
            slot_out = jnp.dot(
                unpack[t * tokens : (t + 1) * tokens, :], oh[:, cols], preferred_element_type=F32
            )
            term = comb[:, t : t + 1] * slot_out
            total = term if total is None else total + term
            terms = part * slot_out
            for k in range(q_w // 128):
                folds[t] = folds[t] + terms[:, k * 128 : (k + 1) * 128]
        mixed[:, cols] = total.astype(BF16)
    for t in range(2):
        high = folds[t].astype(BF16)
        low = (folds[t] - high.astype(F32)).astype(BF16)
        cgs[:, t * tokens : (t + 1) * tokens] = lax.dot_general(
            ones, high, last, preferred_element_type=F32
        ) + lax.dot_general(ones, low, last, preferred_element_type=F32)

    def cg_copy(o):
        return pltpu.make_async_remote_copy(
            src_ref=cgs, dst_ref=cgr.at[o - 1],
            send_sem=cg_send.at[o - 1], recv_sem=cg_recv.at[o - 1],
            device_id=(me, lax.rem(x + o, 4)), device_id_type=MESH,
        )

    for o in range(1, 4):
        cg_copy(o).start()

    pltpu.make_async_copy(bh, bh, home_recv.at[1]).wait()

    def unpack_b(n):
        cols = pl.ds(m(n * 512, 128), 512)
        hg[:, cols] = jnp.dot(
            unpack[...], bh[:rows_n, cols], preferred_element_type=F32
        ) + jnp.dot(unpack[...], bh[rows_n:, cols], preferred_element_type=F32)

    loop(0, hr.shape[1] // 512, unpack_b)
    for o in range(1, 4):
        cg_copy(o).wait_recv()
    cg[...] = cgs[...] + cgr[0] + cgr[1] + cgr[2]

    for o in range(1, 4):
        cg_copy(o).wait_send()
    loop(0, 8, lambda n: wg_copy(n).wait())

    def drain(n):
        g_copy(n).wait_send()
        h_copy(n).wait_send()
        home_b_copy(n).wait_send()
        home_o_copy(n).wait_send()

    loop(1, 32, drain)

    def drain_r(r):
        sib_copy(r).wait_send()
        bsib_copy(r).wait_send()
        for d in range(2):
            xg_copy(r, d).wait_send()
            xf_copy(r, d).wait_send()
            xp_copy(r, d).wait_send()
            xo_copy(r, d).wait_send()

    loop(0, 4, drain_r)


def exchange(pack, unpack, h0, h1, comb, grad, w):
    rows = pack.shape[0]
    tokens, ff = h0.shape
    width = w.shape[1]
    rows_all = 32 * CAP
    vmem = pl.BlockSpec(memory_space=pltpu.VMEM)
    hbm = pl.BlockSpec(memory_space=pl.ANY)
    dma = pltpu.SemaphoreType.DMA
    return pl.pallas_call(
        exchange_kernel,
        out_shape=(
            jax.ShapeDtypeStruct((tokens, width), BF16),
            jax.ShapeDtypeStruct((2 * tokens, ff), F32),
            jax.ShapeDtypeStruct((ff, width), BF16),
            jax.ShapeDtypeStruct((8, 2 * tokens), F32),
        ),
        in_specs=[vmem, vmem, vmem, vmem, vmem, hbm, hbm],
        out_specs=(vmem, vmem, hbm, vmem),
        scratch_shapes=[
            pltpu.VMEM((tokens, width), BF16),
            pltpu.VMEM((rows, ff), BF16),
            pltpu.VMEM((rows, width), BF16),
            pltpu.VMEM((rows, width), BF16),
            pltpu.VMEM((2 * rows, ff), BF16),
            pltpu.VMEM((ff, width), BF16),
            pltpu.VMEM((rows_all, ff), BF16),
            pltpu.VMEM((rows_all, width), BF16),
            pltpu.VMEM((rows_all, width), BF16),
            pltpu.VMEM((2, rows_all // 2, width // 4), BF16),
            pltpu.VMEM((2, rows_all, width // 4), BF16),
            pltpu.VMEM((rows_all, width // 4), BF16),
            pltpu.VMEM((rows_all, ff), BF16),
            pltpu.VMEM((rows_all, ff // 2), BF16),
            pltpu.VMEM((ff, width), BF16),
            pltpu.VMEM((8, 2 * tokens), F32),
            pltpu.VMEM((3, 8, 2 * tokens), F32),
            dma((32,)), dma((32,)), dma((4,)), dma((4,)),
            dma((4, 2)), dma((4, 2)), dma((4, 2)), dma((4, 2)), dma((4,)), dma((4,)),
            dma((4, 2)), dma((4, 2)), dma((4, 2)), dma((4, 2)), dma((4,)), dma((4,)),
            dma((32,)), dma((32,)), dma((2,)), dma((8,)), dma, dma((4,)), dma((3,)), dma((3,)),
        ],
        compiler_params=pltpu.CompilerParams(
            collective_id=0, has_side_effects=True, vmem_limit_bytes=62 * 1024 * 1024
        ),
        cost_estimate=pl.CostEstimate(
            flops=6 * rows_all * ff * width, bytes_accessed=30000000, transcendentals=0
        ),
    )(pack, unpack, h0, h1, comb, grad, w)


def per_device(gate_pre, up_pre, out_grad, combine, expert_ids, down_weight):
    tokens = gate_pre.shape[0]
    width = down_weight.shape[2]
    rows = E * CAP
    flat = jnp.concatenate([expert_ids[:, 0], expert_ids[:, 1]])
    onehot = (flat[:, None] == jnp.arange(E, dtype=jnp.int32)[None, :]).astype(BF16)
    count = tokens * TOP
    before = (jnp.arange(count)[:, None] > jnp.arange(count)[None, :]).astype(BF16)
    earlier = jnp.dot(before, onehot, preferred_element_type=F32)
    position = jnp.sum(earlier * onehot.astype(F32), axis=1).astype(jnp.int32)
    target = flat * CAP + position
    row_ids = jnp.arange(rows, dtype=jnp.int32)
    pack = (target[None, :] == row_ids[:, None]).astype(BF16)
    unpack = (target[:, None] == row_ids[None, :]).astype(BF16)

    gate_f = gate_pre.astype(F32)
    up_f = up_pre.astype(F32)
    sig = jax.nn.sigmoid(gate_f)
    hidden = (gate_f * sig * up_f).astype(BF16)
    mixed, hg, wg, cg = exchange(
        pack, unpack, hidden[:, 0], hidden[:, 1], combine, out_grad, down_weight[0]
    )
    mixed = mixed.reshape(tokens, 4, width // 4)
    combine_grad = jnp.stack([cg[0, :tokens], cg[0, tokens:]], axis=1)
    hidden_grad = jnp.stack([hg[:tokens], hg[tokens:]], axis=1)
    gate_grad = (hidden_grad * up_f * sig * (1.0 + gate_f * (1.0 - sig))).astype(BF16)
    up_grad = (hidden_grad * gate_f * sig).astype(BF16)
    return mixed, combine_grad, gate_grad, up_grad, wg[None]


def solution(mesh):
    return jax.shard_map(
        per_device,
        mesh=mesh,
        in_specs=(
            P("dp", None, "hid"),
            P("dp", None, "hid"),
            P("dp", None),
            P("dp", None),
            P("dp", None),
            P("dp", "hid", None),
        ),
        out_specs=(
            P("dp", None, "hid"),
            P("dp", None),
            P("dp", None, "hid"),
            P("dp", None, "hid"),
            P("dp", "hid", None),
        ),
        check_vma=False,
    )
```

```python
import jax
import jax.numpy as jnp
from jax import lax
from jax.experimental import pallas as pl
from jax.experimental.pallas import tpu as pltpu
from jax.sharding import PartitionSpec as P

E = 8
TOP = 2
CAP = 48
F32 = jnp.float32
BF16 = jnp.bfloat16
MESH = pl.DeviceIdType.MESH


def exchange_kernel(
    slot_row, hidden, comb, grad_hbm, w_hbm, mixed, hg, wg, cg,
    pack, mine, hs, gs, oh, bh, w, hr, gr, os, opx, orx, od, bs, br, wt, cgs, cgr,
    send_h, send_g, recv_h, recv_g, xg_send, xg_recv, xf_send, xf_recv, sib_send, sib_recv,
    xp_send, xp_recv, xo_send, xo_recv, bsib_send, bsib_recv, home_o_send, home_b_send,
    home_recv, wg_sem, w_sem, mine_sem, cg_send, cg_recv,
):
    me = lax.axis_index("dp")
    x = lax.axis_index("hid")
    z = lax.div(me, 8)
    y = lax.rem(lax.div(me, 2), 4)
    core = lax.rem(me, 2)
    e_me = lax.div(me, 4)
    j_me = lax.rem(me, 4)
    sibling = me + 1 - 2 * core
    rows_n = 8 * CAP
    q_w = gr.shape[1] // 4
    half_w = hr.shape[1] // 2

    def m(v, k):
        return pl.multiple_of(v, k)

    def mine_copy(j):
        cols = pl.ds(m(j * 4 * q_w + x * q_w, 128), q_w)
        return pltpu.make_async_copy(
            grad_hbm.at[:, cols], mine.at[:, j * q_w : (j + 1) * q_w], mine_sem.at[j]
        )

    for j in range(4):
        mine_copy(j).start()
    w_copy = pltpu.make_async_copy(w_hbm, w, w_sem)
    w_copy.start()

    barrier = pltpu.get_barrier_semaphore()

    def greet_dp(n, carry):
        peer = lax.rem(me + n, 32)
        pl.semaphore_signal(barrier, inc=1, device_id=(peer, x), device_id_type=MESH)
        return carry

    lax.fori_loop(1, 32, greet_dp, 0)
    for o in range(1, 4):
        pl.semaphore_signal(
            barrier, inc=1, device_id=(me, lax.rem(x + o, 4)), device_id_type=MESH
        )

    tokens = mine.shape[0]
    row_ids = lax.broadcasted_iota(jnp.int32, pack.shape, 0)
    pack[...] = (slot_row[...] == row_ids).astype(F32).astype(BF16)
    diagonal = lax.broadcasted_iota(jnp.int32, (tokens, tokens), 0) == lax.broadcasted_iota(
        jnp.int32, (tokens, tokens), 1
    )

    def weight_of(t):
        return jnp.sum(jnp.where(diagonal, comb[t : t + 1, :], 0.0), axis=1, keepdims=True)

    combine = [weight_of(0), weight_of(1)]
    for j in range(4):
        mine_copy(j).wait()
        cols = slice(j * q_w, (j + 1) * q_w)
        part = mine[:, cols].astype(F32)
        rows = jnp.dot(
            pack[:, :tokens], (combine[0] * part).astype(BF16), preferred_element_type=F32
        ) + jnp.dot(
            pack[:, tokens:], (combine[1] * part).astype(BF16), preferred_element_type=F32
        )
        gs[:, cols] = rows.astype(BF16)
    pl.semaphore_wait(barrier, 34)

    my_half = m(core * half_w, 128)
    other_half = m((1 - core) * half_w, 128)
    my_quarter = m(x * q_w, 128)
    my_expert_rows = m(e_me * CAP, 16)

    def base_of(r):
        return m(r * rows_n, 16)

    def partner(n, sign):
        dz = lax.rem(n, 4)
        dy = lax.rem(dz + lax.div(n, 8), 4)
        dc = lax.rem(lax.div(n, 4), 2)
        pz = lax.rem(z + sign * dz + 4, 4)
        py = lax.rem(y + sign * dy + 4, 4)
        return pz * 8 + py * 2 + lax.rem(core + dc, 2)

    def slot_rows(n, source_core):
        slot = lax.div(n, 8) * 8 + source_core * 4 + lax.rem(n, 4)
        return pl.ds(m(slot * CAP, 16), CAP)

    pltpu.make_async_copy(
        gs.at[pl.ds(my_expert_rows, CAP), pl.ds(m(j_me * q_w, 128), q_w)],
        gr.at[slot_rows(0, core), pl.ds(my_quarter, q_w)],
        recv_g.at[0],
    ).start()

    def g_copy(n):
        p = partner(n, 1)
        return pltpu.make_async_remote_copy(
            src_ref=gs.at[
                pl.ds(m(lax.div(p, 4) * CAP, 16), CAP), pl.ds(m(lax.rem(p, 4) * q_w, 128), q_w)
            ],
            dst_ref=gr.at[slot_rows(n, core), pl.ds(my_quarter, q_w)],
            send_sem=send_g.at[n],
            recv_sem=recv_g.at[lax.div(n, 8)],
            device_id=(p, x),
            device_id_type=MESH,
        )

    def h_copy(n):
        p = partner(n, 1)
        cols = pl.ds(m(lax.rem(p, 2) * half_w, 128), half_w)
        return pltpu.make_async_remote_copy(
            src_ref=hs.at[pl.ds(m(lax.div(p, 4) * CAP, 16), CAP), cols],
            dst_ref=hr.at[slot_rows(n, core), cols],
            send_sem=send_h.at[n],
            recv_sem=recv_h.at[lax.div(n, 8)],
            device_id=(p, x),
            device_id_type=MESH,
        )

    def loop(lo, hi, f):
        def step(n, carry):
            f(n)
            return carry

        lax.fori_loop(lo, hi, step, 0)

    loop(1, 32, lambda n: g_copy(n).start())

    def pack_h(n):
        cols = pl.ds(m(n * 512, 128), 512)
        rows = jnp.dot(pack[:, :tokens], hidden[0, :, cols], preferred_element_type=F32) + jnp.dot(
            pack[:, tokens:], hidden[1, :, cols], preferred_element_type=F32
        )
        hs[:, cols] = rows.astype(BF16)

    loop(0, hr.shape[1] // 512, pack_h)
    pltpu.make_async_copy(
        hs.at[pl.ds(my_expert_rows, CAP), pl.ds(my_half, half_w)],
        hr.at[slot_rows(0, core), pl.ds(my_half, half_w)],
        recv_h.at[0],
    ).start()
    loop(1, 32, lambda n: h_copy(n).start())

    half_rows = rows_n // 2

    def neighbour(d):
        return lax.rem(x + (1, 3)[d], 4)

    def quarter_at(offset):
        return pl.ds(m(lax.rem(x + offset, 4) * q_w, 128), q_w)

    def half_of(r, d):
        return pl.ds(m(r * rows_n + d * half_rows, 16), half_rows)

    def xg_copy(r, d):
        part = gr.at[pl.ds(base_of(r), rows_n), quarter_at(0)]
        return pltpu.make_async_remote_copy(
            src_ref=part, dst_ref=part,
            send_sem=xg_send.at[r, d], recv_sem=xg_recv.at[r, d],
            device_id=(me, neighbour(d)), device_id_type=MESH,
        )

    def xf_copy(r, d):
        part = gr.at[half_of(r, d), quarter_at((3, 1)[d])]
        return pltpu.make_async_remote_copy(
            src_ref=part, dst_ref=part,
            send_sem=xf_send.at[r, d], recv_sem=xf_recv.at[r, d],
            device_id=(me, neighbour(d)), device_id_type=MESH,
        )

    def pass_g(r):
        part = gr.at[pl.ds(base_of(r), rows_n), quarter_at(0)]
        pltpu.make_async_copy(part, part, recv_g.at[r]).wait()
        for d in range(2):
            xg_copy(r, d).start()

    def forward_g(r):
        for d in range(2):
            part = gr.at[pl.ds(base_of(r), rows_n), quarter_at((3, 1)[d])]
            pltpu.make_async_copy(part, part, xg_recv.at[r, d]).wait()
            xf_copy(r, d).start()

    def sib_copy(r):
        part = hr.at[pl.ds(base_of(r), rows_n), pl.ds(my_half, half_w)]
        return pltpu.make_async_remote_copy(
            src_ref=part, dst_ref=part, send_sem=sib_send.at[r], recv_sem=sib_recv.at[r],
            device_id=(sibling, x), device_id_type=MESH,
        )

    def pass_h(r):
        part = hr.at[pl.ds(base_of(r), rows_n), pl.ds(my_half, half_w)]
        pltpu.make_async_copy(part, part, recv_h.at[r]).wait()
        sib_copy(r).start()

    def xp_copy(r, d):
        return pltpu.make_async_remote_copy(
            src_ref=os.at[half_of(r, d), quarter_at(2)],
            dst_ref=opx.at[d, pl.ds(m(r * half_rows, 16), half_rows), :],
            send_sem=xp_send.at[r, d], recv_sem=xp_recv.at[r, d],
            device_id=(me, neighbour(d)), device_id_type=MESH,
        )

    def xo_copy(r, d):
        return pltpu.make_async_remote_copy(
            src_ref=os.at[pl.ds(base_of(r), rows_n), quarter_at((1, 3)[d])],
            dst_ref=orx.at[d, pl.ds(base_of(r), rows_n), :],
            send_sem=xo_send.at[r, d], recv_sem=xo_recv.at[r, d],
            device_id=(me, neighbour(d)), device_id_type=MESH,
        )

    def pass_out(r):
        for d in range(2):
            part = opx.at[d, pl.ds(m(r * half_rows, 16), half_rows), :]
            pltpu.make_async_copy(part, part, xp_recv.at[r, d]).wait()

            def tile(i):
                sub = pl.ds(m(r * rows_n + d * half_rows + i * CAP, 16), CAP)
                come = opx[d, pl.ds(m(r * half_rows + i * CAP, 16), CAP), :]
                cols = quarter_at((1, 3)[d])
                os[sub, cols] = (os[sub, cols].astype(F32) + come.astype(F32)).astype(BF16)

            loop(0, half_rows // CAP, tile)
            xo_copy(r, d).start()

    def out_product(r):
        part = hr.at[pl.ds(base_of(r), rows_n), pl.ds(other_half, half_w)]
        pltpu.make_async_copy(part, part, sib_recv.at[r]).wait()
        rows = pl.ds(base_of(r), rows_n)

        def tile(q):
            cols = pl.ds(m(q * 2 * q_w, 128), 2 * q_w)
            acc = jnp.dot(hr[rows, :], w[:, cols], preferred_element_type=F32)
            os[rows, cols] = acc.astype(BF16)

        loop(0, 2, tile)
        for d in range(2):
            xp_copy(r, d).start()

    def bsib_copy(r):
        rows = pl.ds(base_of(r), rows_n)
        return pltpu.make_async_remote_copy(
            src_ref=bs.at[rows, pl.ds(other_half, half_w)],
            dst_ref=br.at[rows, :],
            send_sem=bsib_send.at[r], recv_sem=bsib_recv.at[r],
            device_id=(sibling, x), device_id_type=MESH,
        )

    def back_product(r):
        for d in range(2):
            part = gr.at[half_of(r, d), quarter_at(2)]
            pltpu.make_async_copy(part, part, xf_recv.at[r, d]).wait()
        rows = pl.ds(base_of(r), rows_n)

        def tile(n):
            cols = pl.ds(m(n * 512, 128), 512)
            acc = lax.dot_general(
                gr[rows, :], w[cols, :], (((1,), (1,)), ((), ())), preferred_element_type=F32
            )
            bs[rows, cols] = acc.astype(BF16)

        loop(0, 4, tile)
        bsib_copy(r).start()

    def home_b_copy(n):
        p = partner(n, -1)
        return pltpu.make_async_remote_copy(
            src_ref=br.at[slot_rows(n, lax.rem(p, 2)), :],
            dst_ref=bh.at[
                pl.ds(m((lax.div(j_me, 2) * E + e_me) * CAP, 16), CAP), pl.ds(my_half, half_w)
            ],
            send_sem=home_b_send.at[n], recv_sem=home_recv.at[1],
            device_id=(p, x), device_id_type=MESH,
        )

    def home_o_copy(n):
        p = partner(n, -1)
        return pltpu.make_async_remote_copy(
            src_ref=od.at[slot_rows(n, lax.rem(p, 2)), :],
            dst_ref=oh.at[pl.ds(my_expert_rows, CAP), pl.ds(m(j_me * q_w, 128), q_w)],
            send_sem=home_o_send.at[n], recv_sem=home_recv.at[0],
            device_id=(p, x), device_id_type=MESH,
        )

    def back_sum(r):
        rows = pl.ds(base_of(r), rows_n)
        part = br.at[rows, :]
        pltpu.make_async_copy(part, part, bsib_recv.at[r]).wait()

        def tile(i):
            sub = pl.ds(m(base_of(r) + i * CAP, 16), CAP)
            total = br[sub, :].astype(F32) + bs[sub, pl.ds(my_half, half_w)].astype(F32)
            br[sub, :] = total.astype(BF16)

        loop(0, 8, tile)

    def out_sum(r):
        for d in range(2):
            part = orx.at[d, pl.ds(base_of(r), rows_n), :]
            pltpu.make_async_copy(part, part, xo_recv.at[r, d]).wait()

        def tile(i):
            sub = pl.ds(m(base_of(r) + i * CAP, 16), CAP)
            total = os[sub, pl.ds(my_quarter, q_w)].astype(F32)
            for k in range(2):
                total = total + orx[k, sub, :].astype(F32)
            od[sub, :] = total.astype(BF16)

        loop(0, 8, tile)

    def wg_copy(n):
        rows = pl.ds(m(n * 256, 16), 256)
        return pltpu.make_async_copy(wt.at[rows, :], wg.at[rows, :], wg_sem.at[n])

    def wg_tile(n):
        cols = pl.ds(m(n * 256, 128), 256)
        acc = lax.dot_general(
            hr[:, cols], gr[...], (((0,), (0,)), ((), ())), preferred_element_type=F32
        )
        wt[pl.ds(m(n * 256, 16), 256), :] = acc.astype(BF16)
        wg_copy(n).start()

    def home_b(r):
        back_sum(r)

        @pl.when(r == 0)
        def _():
            pltpu.make_async_copy(
                br.at[slot_rows(0, core), :],
                bh.at[
                    pl.ds(m((lax.div(j_me, 2) * E + e_me) * CAP, 16), CAP), pl.ds(my_half, half_w)
                ],
                home_recv.at[1],
            ).start()

        loop(jnp.maximum(r * 8, 1), r * 8 + 8, lambda n: home_b_copy(n).start())

    def home_o(r):
        out_sum(r)

        @pl.when(r == 0)
        def _():
            pltpu.make_async_copy(
                od.at[slot_rows(0, core), :],
                oh.at[pl.ds(my_expert_rows, CAP), pl.ds(m(j_me * q_w, 128), q_w)],
                home_recv.at[0],
            ).start()

        loop(jnp.maximum(r * 8, 1), r * 8 + 8, lambda n: home_o_copy(n).start())

    pass_g(0)
    pass_g(1)
    forward_g(0)
    w_copy.wait()

    def step(r):
        @pl.when(r < 2)
        def _():
            pass_g(r + 2)

        @pl.when(r < 3)
        def _():
            forward_g(r + 1)

        @pl.when(r < 4)
        def _():
            pass_h(r)

        @pl.when((r > 0) & (r < 5))
        def _():
            home_b(r - 1)

        @pl.when(r > 1)
        def _():
            home_o(r - 2)

        @pl.when(r < 4)
        def _():
            out_product(r)
            back_product(r)
            pass_out(r)

        @pl.when(r > 3)
        def _():
            loop(r * 4 - 16, r * 4 - 12, wg_tile)

    loop(0, 6, step)

    pltpu.make_async_copy(oh, oh, home_recv.at[0]).wait()
    def unpack(t, rows):
        return lax.dot_general(
            pack[:, t * tokens : (t + 1) * tokens], rows, (((0,), (0,)), ((), ())),
            preferred_element_type=F32,
        )

    ones = jnp.ones((8, 128), BF16)
    last = (((1,), (1,)), ((), ()))
    folds = [jnp.zeros((tokens, 128), F32), jnp.zeros((tokens, 128), F32)]
    for j in range(4):
        cols = slice(j * q_w, (j + 1) * q_w)
        part = mine[:, cols].astype(F32)
        total = None
        for t in range(2):
            slot_out = unpack(t, oh[:, cols])
            term = combine[t] * slot_out
            total = term if total is None else total + term
            terms = part * slot_out
            for k in range(q_w // 128):
                folds[t] = folds[t] + terms[:, k * 128 : (k + 1) * 128]
        mixed[j] = total.astype(BF16)
    for t in range(2):
        high = folds[t].astype(BF16)
        low = (folds[t] - high.astype(F32)).astype(BF16)
        cgs[t * 8 : (t + 1) * 8, :] = lax.dot_general(
            ones, high, last, preferred_element_type=F32
        ) + lax.dot_general(ones, low, last, preferred_element_type=F32)

    def cg_copy(o):
        return pltpu.make_async_remote_copy(
            src_ref=cgs, dst_ref=cgr.at[o - 1],
            send_sem=cg_send.at[o - 1], recv_sem=cg_recv.at[o - 1],
            device_id=(me, lax.rem(x + o, 4)), device_id_type=MESH,
        )

    for o in range(1, 4):
        cg_copy(o).start()

    pltpu.make_async_copy(bh, bh, home_recv.at[1]).wait()

    def unpack_b(n):
        cols = pl.ds(m(n * 512, 128), 512)
        for t in range(2):
            hg[t, :, cols] = unpack(t, bh[:rows_n, cols]) + unpack(t, bh[rows_n:, cols])

    loop(0, hr.shape[1] // 512, unpack_b)
    for o in range(1, 4):
        cg_copy(o).wait_recv()
    total = cgs[...] + cgr[0] + cgr[1] + cgr[2]
    cg[0:1, :] = total[0:1, :]
    cg[1:2, :] = total[8:9, :]

    for o in range(1, 4):
        cg_copy(o).wait_send()
    loop(0, 8, lambda n: wg_copy(n).wait())

    def drain(n):
        g_copy(n).wait_send()
        h_copy(n).wait_send()
        home_b_copy(n).wait_send()
        home_o_copy(n).wait_send()

    loop(1, 32, drain)

    def drain_r(r):
        sib_copy(r).wait_send()
        bsib_copy(r).wait_send()
        for d in range(2):
            xg_copy(r, d).wait_send()
            xf_copy(r, d).wait_send()
            xp_copy(r, d).wait_send()
            xo_copy(r, d).wait_send()

    loop(0, 4, drain_r)


def exchange(slot_row, hidden, comb, grad, w):
    rows = E * CAP
    _, tokens, ff = hidden.shape
    width = w.shape[1]
    rows_all = 32 * CAP
    vmem = pl.BlockSpec(memory_space=pltpu.VMEM)
    hbm = pl.BlockSpec(memory_space=pl.ANY)
    dma = pltpu.SemaphoreType.DMA
    return pl.pallas_call(
        exchange_kernel,
        out_shape=(
            jax.ShapeDtypeStruct((4, tokens, width // 4), BF16),
            jax.ShapeDtypeStruct((2, tokens, ff), F32),
            jax.ShapeDtypeStruct((ff, width), BF16),
            jax.ShapeDtypeStruct((2, tokens), F32),
        ),
        in_specs=[vmem, vmem, vmem, hbm, hbm],
        out_specs=(vmem, vmem, hbm, vmem),
        scratch_shapes=[
            pltpu.VMEM((rows, 2 * tokens), BF16),
            pltpu.VMEM((tokens, width), BF16),
            pltpu.VMEM((rows, ff), BF16),
            pltpu.VMEM((rows, width), BF16),
            pltpu.VMEM((rows, width), BF16),
            pltpu.VMEM((2 * rows, ff), BF16),
            pltpu.VMEM((ff, width), BF16),
            pltpu.VMEM((rows_all, ff), BF16),
            pltpu.VMEM((rows_all, width), BF16),
            pltpu.VMEM((rows_all, width), BF16),
            pltpu.VMEM((2, rows_all // 2, width // 4), BF16),
            pltpu.VMEM((2, rows_all, width // 4), BF16),
            pltpu.VMEM((rows_all, width // 4), BF16),
            pltpu.VMEM((rows_all, ff), BF16),
            pltpu.VMEM((rows_all, ff // 2), BF16),
            pltpu.VMEM((ff, width), BF16),
            pltpu.VMEM((16, tokens), F32),
            pltpu.VMEM((3, 16, tokens), F32),
            dma((32,)), dma((32,)), dma((4,)), dma((4,)),
            dma((4, 2)), dma((4, 2)), dma((4, 2)), dma((4, 2)), dma((4,)), dma((4,)),
            dma((4, 2)), dma((4, 2)), dma((4, 2)), dma((4, 2)), dma((4,)), dma((4,)),
            dma((32,)), dma((32,)), dma((2,)), dma((8,)), dma, dma((4,)), dma((3,)), dma((3,)),
        ],
        compiler_params=pltpu.CompilerParams(
            collective_id=0, has_side_effects=True, vmem_limit_bytes=62 * 1024 * 1024
        ),
        cost_estimate=pl.CostEstimate(
            flops=6 * rows_all * ff * width, bytes_accessed=30000000, transcendentals=0
        ),
    )(slot_row, hidden, comb, grad, w)


def per_device(gate_pre, up_pre, out_grad, combine, expert_ids, down_weight):
    tokens = gate_pre.shape[0]
    width = down_weight.shape[2]
    flat = jnp.concatenate([expert_ids[:, 0], expert_ids[:, 1]])
    onehot = (flat[:, None] == jnp.arange(E, dtype=jnp.int32)[None, :]).astype(BF16)
    count = tokens * TOP
    before = (jnp.arange(count)[:, None] > jnp.arange(count)[None, :]).astype(BF16)
    earlier = jnp.dot(before, onehot, preferred_element_type=F32)
    position = jnp.sum(earlier * onehot.astype(F32), axis=1).astype(jnp.int32)
    slot_row = (flat * CAP + position).reshape(1, count)

    gate_f = gate_pre.astype(F32)
    up_f = up_pre.astype(F32)
    sig = jax.nn.sigmoid(gate_f)
    hidden = (gate_f * sig * up_f).astype(BF16)
    mixed, hg, wg, cg = exchange(
        slot_row, jnp.transpose(hidden, (1, 0, 2)), combine.T, out_grad, down_weight[0]
    )
    mixed = jnp.transpose(mixed, (1, 0, 2))
    combine_grad = cg.T
    hidden_grad = jnp.transpose(hg, (1, 0, 2))
    gate_grad = (hidden_grad * up_f * sig * (1.0 + gate_f * (1.0 - sig))).astype(BF16)
    up_grad = (hidden_grad * gate_f * sig).astype(BF16)
    return mixed, combine_grad, gate_grad, up_grad, wg[None]


def solution(mesh):
    return jax.shard_map(
        per_device,
        mesh=mesh,
        in_specs=(
            P("dp", None, "hid"),
            P("dp", None, "hid"),
            P("dp", None),
            P("dp", None),
            P("dp", None),
            P("dp", "hid", None),
        ),
        out_specs=(
            P("dp", None, "hid"),
            P("dp", None),
            P("dp", None, "hid"),
            P("dp", None, "hid"),
            P("dp", "hid", None),
        ),
        check_vma=False,
    )
```

```python
import jax
import jax.numpy as jnp
from jax import lax
from jax.experimental import pallas as pl
from jax.experimental.pallas import tpu as pltpu
from jax.sharding import PartitionSpec as P

E = 8
TOP = 2
CAP = 48
F32 = jnp.float32
BF16 = jnp.bfloat16
MESH = pl.DeviceIdType.MESH


def exchange_kernel(
    slot_row, hidden, comb, grad_hbm, w_hbm, mixed, hg, wg, cg,
    pack, mine, hs, gs, oh, bh, w, hr, gr, os, opx, orx, od, bs, br, wt, cgs, cgr,
    send_h, send_g, recv_h, recv_g, xg_send, xg_recv, xf_send, xf_recv, sib_send, sib_recv,
    xp_send, xp_recv, xo_send, xo_recv, bsib_send, bsib_recv, home_o_send, home_b_send,
    home_recv, wg_sem, w_sem, mine_sem, cg_send, cg_recv,
):
    me = lax.axis_index("dp")
    x = lax.axis_index("hid")
    z = lax.div(me, 8)
    y = lax.rem(lax.div(me, 2), 4)
    core = lax.rem(me, 2)
    e_me = lax.div(me, 4)
    j_me = lax.rem(me, 4)
    sibling = me + 1 - 2 * core
    rows_n = 8 * CAP
    q_w = gr.shape[1] // 4
    half_w = hr.shape[1] // 2

    def m(v, k):
        return pl.multiple_of(v, k)

    def mine_copy(j):
        cols = pl.ds(m(j * 4 * q_w + x * q_w, 128), q_w)
        return pltpu.make_async_copy(
            grad_hbm.at[:, cols], mine.at[:, j * q_w : (j + 1) * q_w], mine_sem.at[j]
        )

    for j in range(4):
        mine_copy(j).start()
    w_copy = pltpu.make_async_copy(w_hbm, w, w_sem)
    w_copy.start()

    barrier = pltpu.get_barrier_semaphore()

    def greet_dp(n, carry):
        peer = lax.rem(me + n, 32)
        pl.semaphore_signal(barrier, inc=1, device_id=(peer, x), device_id_type=MESH)
        return carry

    lax.fori_loop(1, 32, greet_dp, 0)
    for o in range(1, 4):
        pl.semaphore_signal(
            barrier, inc=1, device_id=(me, lax.rem(x + o, 4)), device_id_type=MESH
        )

    tokens = mine.shape[0]
    row_ids = lax.broadcasted_iota(jnp.int32, pack.shape, 0)
    pack[...] = (slot_row[...] == row_ids).astype(F32).astype(BF16)
    diagonal = lax.broadcasted_iota(jnp.int32, (tokens, tokens), 0) == lax.broadcasted_iota(
        jnp.int32, (tokens, tokens), 1
    )

    def weight_of(t):
        return jnp.sum(jnp.where(diagonal, comb[t : t + 1, :], 0.0), axis=1, keepdims=True)

    combine = [weight_of(0), weight_of(1)]
    for j in range(4):
        mine_copy(j).wait()
        cols = slice(j * q_w, (j + 1) * q_w)
        part = mine[:, cols].astype(F32)
        rows = jnp.dot(
            pack[:, :tokens], (combine[0] * part).astype(BF16), preferred_element_type=F32
        ) + jnp.dot(
            pack[:, tokens:], (combine[1] * part).astype(BF16), preferred_element_type=F32
        )
        gs[:, cols] = rows.astype(BF16)
    pl.semaphore_wait(barrier, 34)

    my_half = m(core * half_w, 128)
    other_half = m((1 - core) * half_w, 128)
    my_quarter = m(x * q_w, 128)
    my_expert_rows = m(e_me * CAP, 16)

    def base_of(r):
        return m(r * rows_n, 16)

    def partner(n, sign):
        dz = lax.rem(n, 4)
        dy = lax.rem(dz + lax.div(n, 8), 4)
        dc = lax.rem(lax.div(n, 4), 2)
        pz = lax.rem(z + sign * dz + 4, 4)
        py = lax.rem(y + sign * dy + 4, 4)
        return pz * 8 + py * 2 + lax.rem(core + dc, 2)

    def slot_rows(n, source_core):
        slot = lax.div(n, 8) * 8 + source_core * 4 + lax.rem(n, 4)
        return pl.ds(m(slot * CAP, 16), CAP)

    pltpu.make_async_copy(
        gs.at[pl.ds(my_expert_rows, CAP), pl.ds(m(j_me * q_w, 128), q_w)],
        gr.at[slot_rows(0, core), pl.ds(my_quarter, q_w)],
        recv_g.at[0],
    ).start()

    def g_copy(n):
        p = partner(n, 1)
        return pltpu.make_async_remote_copy(
            src_ref=gs.at[
                pl.ds(m(lax.div(p, 4) * CAP, 16), CAP), pl.ds(m(lax.rem(p, 4) * q_w, 128), q_w)
            ],
            dst_ref=gr.at[slot_rows(n, core), pl.ds(my_quarter, q_w)],
            send_sem=send_g.at[n],
            recv_sem=recv_g.at[lax.div(n, 8)],
            device_id=(p, x),
            device_id_type=MESH,
        )

    def h_copy(n):
        p = partner(n, 1)
        cols = pl.ds(m(lax.rem(p, 2) * half_w, 128), half_w)
        return pltpu.make_async_remote_copy(
            src_ref=hs.at[pl.ds(m(lax.div(p, 4) * CAP, 16), CAP), cols],
            dst_ref=hr.at[slot_rows(n, core), cols],
            send_sem=send_h.at[n],
            recv_sem=recv_h.at[lax.div(n, 8)],
            device_id=(p, x),
            device_id_type=MESH,
        )

    def loop(lo, hi, f):
        def step(n, carry):
            f(n)
            return carry

        lax.fori_loop(lo, hi, step, 0)

    loop(1, 32, lambda n: g_copy(n).start())

    def pack_h(n):
        cols = pl.ds(m(n * 512, 128), 512)
        rows = jnp.dot(pack[:, :tokens], hidden[0, :, cols], preferred_element_type=F32) + jnp.dot(
            pack[:, tokens:], hidden[1, :, cols], preferred_element_type=F32
        )
        hs[:, cols] = rows.astype(BF16)

    loop(0, hr.shape[1] // 512, pack_h)
    pltpu.make_async_copy(
        hs.at[pl.ds(my_expert_rows, CAP), pl.ds(my_half, half_w)],
        hr.at[slot_rows(0, core), pl.ds(my_half, half_w)],
        recv_h.at[0],
    ).start()
    loop(1, 32, lambda n: h_copy(n).start())

    half_rows = rows_n // 2

    def neighbour(d):
        return lax.rem(x + (1, 3)[d], 4)

    def quarter_at(offset):
        return pl.ds(m(lax.rem(x + offset, 4) * q_w, 128), q_w)

    def half_of(r, d):
        return pl.ds(m(r * rows_n + d * half_rows, 16), half_rows)

    def xg_copy(r, d):
        part = gr.at[pl.ds(base_of(r), rows_n), quarter_at(0)]
        return pltpu.make_async_remote_copy(
            src_ref=part, dst_ref=part,
            send_sem=xg_send.at[r, d], recv_sem=xg_recv.at[r, d],
            device_id=(me, neighbour(d)), device_id_type=MESH,
        )

    def xf_copy(r, d):
        part = gr.at[half_of(r, d), quarter_at((3, 1)[d])]
        return pltpu.make_async_remote_copy(
            src_ref=part, dst_ref=part,
            send_sem=xf_send.at[r, d], recv_sem=xf_recv.at[r, d],
            device_id=(me, neighbour(d)), device_id_type=MESH,
        )

    def pass_g(r):
        part = gr.at[pl.ds(base_of(r), rows_n), quarter_at(0)]
        pltpu.make_async_copy(part, part, recv_g.at[r]).wait()
        for d in range(2):
            xg_copy(r, d).start()

    def forward_g(r):
        for d in range(2):
            part = gr.at[pl.ds(base_of(r), rows_n), quarter_at((3, 1)[d])]
            pltpu.make_async_copy(part, part, xg_recv.at[r, d]).wait()
            xf_copy(r, d).start()

    def sib_copy(r):
        part = hr.at[pl.ds(base_of(r), rows_n), pl.ds(my_half, half_w)]
        return pltpu.make_async_remote_copy(
            src_ref=part, dst_ref=part, send_sem=sib_send.at[r], recv_sem=sib_recv.at[r],
            device_id=(sibling, x), device_id_type=MESH,
        )

    def pass_h(r):
        part = hr.at[pl.ds(base_of(r), rows_n), pl.ds(my_half, half_w)]
        pltpu.make_async_copy(part, part, recv_h.at[r]).wait()
        sib_copy(r).start()

    def xp_copy(r, d):
        return pltpu.make_async_remote_copy(
            src_ref=os.at[half_of(r, d), quarter_at(2)],
            dst_ref=opx.at[d, pl.ds(m(r * half_rows, 16), half_rows), :],
            send_sem=xp_send.at[r, d], recv_sem=xp_recv.at[r, d],
            device_id=(me, neighbour(d)), device_id_type=MESH,
        )

    def xo_copy(r, d):
        return pltpu.make_async_remote_copy(
            src_ref=os.at[pl.ds(base_of(r), rows_n), quarter_at((1, 3)[d])],
            dst_ref=orx.at[d, pl.ds(base_of(r), rows_n), :],
            send_sem=xo_send.at[r, d], recv_sem=xo_recv.at[r, d],
            device_id=(me, neighbour(d)), device_id_type=MESH,
        )

    def pass_out(r):
        for d in range(2):
            part = opx.at[d, pl.ds(m(r * half_rows, 16), half_rows), :]
            pltpu.make_async_copy(part, part, xp_recv.at[r, d]).wait()

            def tile(i):
                sub = pl.ds(m(r * rows_n + d * half_rows + i * CAP, 16), CAP)
                come = opx[d, pl.ds(m(r * half_rows + i * CAP, 16), CAP), :]
                cols = quarter_at((1, 3)[d])
                os[sub, cols] = (os[sub, cols].astype(F32) + come.astype(F32)).astype(BF16)

            loop(0, half_rows // CAP, tile)
            xo_copy(r, d).start()

    def out_product(r):
        part = hr.at[pl.ds(base_of(r), rows_n), pl.ds(other_half, half_w)]
        pltpu.make_async_copy(part, part, sib_recv.at[r]).wait()
        rows = pl.ds(base_of(r), rows_n)

        def tile(q):
            cols = pl.ds(m(q * 2 * q_w, 128), 2 * q_w)
            acc = jnp.dot(hr[rows, :], w[:, cols], preferred_element_type=F32)
            os[rows, cols] = acc.astype(BF16)

        loop(0, 2, tile)
        for d in range(2):
            xp_copy(r, d).start()

    def bsib_copy(r):
        rows = pl.ds(base_of(r), rows_n)
        return pltpu.make_async_remote_copy(
            src_ref=bs.at[rows, pl.ds(other_half, half_w)],
            dst_ref=br.at[rows, :],
            send_sem=bsib_send.at[r], recv_sem=bsib_recv.at[r],
            device_id=(sibling, x), device_id_type=MESH,
        )

    def back_product(r):
        for d in range(2):
            part = gr.at[half_of(r, d), quarter_at(2)]
            pltpu.make_async_copy(part, part, xf_recv.at[r, d]).wait()
        rows = pl.ds(base_of(r), rows_n)

        def tile(n):
            cols = pl.ds(m(n * 512, 128), 512)
            acc = lax.dot_general(
                gr[rows, :], w[cols, :], (((1,), (1,)), ((), ())), preferred_element_type=F32
            )
            bs[rows, cols] = acc.astype(BF16)

        loop(0, 4, tile)
        bsib_copy(r).start()

    def home_b_copy(n):
        p = partner(n, -1)
        return pltpu.make_async_remote_copy(
            src_ref=br.at[slot_rows(n, lax.rem(p, 2)), :],
            dst_ref=bh.at[
                pl.ds(m((lax.div(j_me, 2) * E + e_me) * CAP, 16), CAP), pl.ds(my_half, half_w)
            ],
            send_sem=home_b_send.at[n], recv_sem=home_recv.at[1],
            device_id=(p, x), device_id_type=MESH,
        )

    def home_o_copy(n):
        p = partner(n, -1)
        return pltpu.make_async_remote_copy(
            src_ref=od.at[slot_rows(n, lax.rem(p, 2)), :],
            dst_ref=oh.at[pl.ds(my_expert_rows, CAP), pl.ds(m(j_me * q_w, 128), q_w)],
            send_sem=home_o_send.at[n], recv_sem=home_recv.at[0],
            device_id=(p, x), device_id_type=MESH,
        )

    def back_sum(r):
        rows = pl.ds(base_of(r), rows_n)
        part = br.at[rows, :]
        pltpu.make_async_copy(part, part, bsib_recv.at[r]).wait()

        def tile(i):
            sub = pl.ds(m(base_of(r) + i * CAP, 16), CAP)
            total = br[sub, :].astype(F32) + bs[sub, pl.ds(my_half, half_w)].astype(F32)
            br[sub, :] = total.astype(BF16)

        loop(0, 8, tile)

    def out_sum(r):
        for d in range(2):
            part = orx.at[d, pl.ds(base_of(r), rows_n), :]
            pltpu.make_async_copy(part, part, xo_recv.at[r, d]).wait()

        def tile(i):
            sub = pl.ds(m(base_of(r) + i * CAP, 16), CAP)
            total = os[sub, pl.ds(my_quarter, q_w)].astype(F32)
            for k in range(2):
                total = total + orx[k, sub, :].astype(F32)
            od[sub, :] = total.astype(BF16)

        loop(0, 8, tile)

    def wg_copy(n):
        rows = pl.ds(m(n * 256, 16), 256)
        return pltpu.make_async_copy(wt.at[rows, :], wg.at[rows, :], wg_sem.at[n])

    def wg_tile(n):
        cols = pl.ds(m(n * 256, 128), 256)
        acc = lax.dot_general(
            hr[:, cols], gr[...], (((0,), (0,)), ((), ())), preferred_element_type=F32
        )
        wt[pl.ds(m(n * 256, 16), 256), :] = acc.astype(BF16)
        wg_copy(n).start()

    def home_b(r):
        back_sum(r)

        @pl.when(r == 0)
        def _():
            pltpu.make_async_copy(
                br.at[slot_rows(0, core), :],
                bh.at[
                    pl.ds(m((lax.div(j_me, 2) * E + e_me) * CAP, 16), CAP), pl.ds(my_half, half_w)
                ],
                home_recv.at[1],
            ).start()

        loop(jnp.maximum(r * 8, 1), r * 8 + 8, lambda n: home_b_copy(n).start())

    def home_o(r):
        out_sum(r)

        @pl.when(r == 0)
        def _():
            pltpu.make_async_copy(
                od.at[slot_rows(0, core), :],
                oh.at[pl.ds(my_expert_rows, CAP), pl.ds(m(j_me * q_w, 128), q_w)],
                home_recv.at[0],
            ).start()

        loop(jnp.maximum(r * 8, 1), r * 8 + 8, lambda n: home_o_copy(n).start())

    pass_g(0)
    pass_g(1)
    forward_g(0)
    w_copy.wait()

    def step(r):
        @pl.when(r < 2)
        def _():
            pass_g(r + 2)

        @pl.when(r < 3)
        def _():
            forward_g(r + 1)

        @pl.when(r < 4)
        def _():
            pass_h(r)

        @pl.when((r > 0) & (r < 5))
        def _():
            home_b(r - 1)

        @pl.when(r > 1)
        def _():
            home_o(r - 2)

        @pl.when(r < 4)
        def _():
            out_product(r)
            back_product(r)
            pass_out(r)

        @pl.when(r > 3)
        def _():
            loop(r * 4 - 16, r * 4 - 12, wg_tile)

    loop(0, 6, step)

    pltpu.make_async_copy(oh, oh, home_recv.at[0]).wait()
    def unpack(t, rows):
        return lax.dot_general(
            pack[:, t * tokens : (t + 1) * tokens], rows, (((0,), (0,)), ((), ())),
            preferred_element_type=F32,
        )

    ones = jnp.ones((8, 128), BF16)
    last = (((1,), (1,)), ((), ()))
    slices = []
    folds = [jnp.zeros((tokens, 128), F32), jnp.zeros((tokens, 128), F32)]
    for j in range(4):
        cols = slice(j * q_w, (j + 1) * q_w)
        part = mine[:, cols].astype(F32)
        total = None
        for t in range(2):
            slot_out = unpack(t, oh[:, cols])
            term = combine[t] * slot_out
            total = term if total is None else total + term
            terms = part * slot_out
            for k in range(q_w // 128):
                folds[t] = folds[t] + terms[:, k * 128 : (k + 1) * 128]
        slices.append(total)
    for t in range(2):
        high = folds[t].astype(BF16)
        low = (folds[t] - high.astype(F32)).astype(BF16)
        cgs[t * 8 : (t + 1) * 8, :] = lax.dot_general(
            ones, high, last, preferred_element_type=F32
        ) + lax.dot_general(ones, low, last, preferred_element_type=F32)

    def cg_copy(o):
        return pltpu.make_async_remote_copy(
            src_ref=cgs, dst_ref=cgr.at[o - 1],
            send_sem=cg_send.at[o - 1], recv_sem=cg_recv.at[o - 1],
            device_id=(me, lax.rem(x + o, 4)), device_id_type=MESH,
        )

    for o in range(1, 4):
        cg_copy(o).start()
    mixed[...] = jnp.stack(slices, axis=1).astype(BF16)

    pltpu.make_async_copy(bh, bh, home_recv.at[1]).wait()

    def unpack_b(n):
        cols = pl.ds(m(n * 512, 128), 512)
        for t in range(2):
            hg[t, :, cols] = unpack(t, bh[:rows_n, cols]) + unpack(t, bh[rows_n:, cols])

    loop(0, hr.shape[1] // 512, unpack_b)
    for o in range(1, 4):
        cg_copy(o).wait_recv()
    total = cgs[...] + cgr[0] + cgr[1] + cgr[2]
    cg[0:1, :] = total[0:1, :]
    cg[1:2, :] = total[8:9, :]

    for o in range(1, 4):
        cg_copy(o).wait_send()
    loop(0, 8, lambda n: wg_copy(n).wait())

    def drain(n):
        g_copy(n).wait_send()
        h_copy(n).wait_send()
        home_b_copy(n).wait_send()
        home_o_copy(n).wait_send()

    loop(1, 32, drain)

    def drain_r(r):
        sib_copy(r).wait_send()
        bsib_copy(r).wait_send()
        for d in range(2):
            xg_copy(r, d).wait_send()
            xf_copy(r, d).wait_send()
            xp_copy(r, d).wait_send()
            xo_copy(r, d).wait_send()

    loop(0, 4, drain_r)


def exchange(slot_row, hidden, comb, grad, w):
    rows = E * CAP
    _, tokens, ff = hidden.shape
    width = w.shape[1]
    rows_all = 32 * CAP
    vmem = pl.BlockSpec(memory_space=pltpu.VMEM)
    hbm = pl.BlockSpec(memory_space=pl.ANY)
    dma = pltpu.SemaphoreType.DMA
    return pl.pallas_call(
        exchange_kernel,
        out_shape=(
            jax.ShapeDtypeStruct((tokens, 4, width // 4), BF16),
            jax.ShapeDtypeStruct((2, tokens, ff), F32),
            jax.ShapeDtypeStruct((ff, width), BF16),
            jax.ShapeDtypeStruct((2, tokens), F32),
        ),
        in_specs=[vmem, vmem, vmem, hbm, hbm],
        out_specs=(vmem, vmem, hbm, vmem),
        scratch_shapes=[
            pltpu.VMEM((rows, 2 * tokens), BF16),
            pltpu.VMEM((tokens, width), BF16),
            pltpu.VMEM((rows, ff), BF16),
            pltpu.VMEM((rows, width), BF16),
            pltpu.VMEM((rows, width), BF16),
            pltpu.VMEM((2 * rows, ff), BF16),
            pltpu.VMEM((ff, width), BF16),
            pltpu.VMEM((rows_all, ff), BF16),
            pltpu.VMEM((rows_all, width), BF16),
            pltpu.VMEM((rows_all, width), BF16),
            pltpu.VMEM((2, rows_all // 2, width // 4), BF16),
            pltpu.VMEM((2, rows_all, width // 4), BF16),
            pltpu.VMEM((rows_all, width // 4), BF16),
            pltpu.VMEM((rows_all, ff), BF16),
            pltpu.VMEM((rows_all, ff // 2), BF16),
            pltpu.VMEM((ff, width), BF16),
            pltpu.VMEM((16, tokens), F32),
            pltpu.VMEM((3, 16, tokens), F32),
            dma((32,)), dma((32,)), dma((4,)), dma((4,)),
            dma((4, 2)), dma((4, 2)), dma((4, 2)), dma((4, 2)), dma((4,)), dma((4,)),
            dma((4, 2)), dma((4, 2)), dma((4, 2)), dma((4, 2)), dma((4,)), dma((4,)),
            dma((32,)), dma((32,)), dma((2,)), dma((8,)), dma, dma((4,)), dma((3,)), dma((3,)),
        ],
        compiler_params=pltpu.CompilerParams(
            collective_id=0, has_side_effects=True, vmem_limit_bytes=62 * 1024 * 1024
        ),
        cost_estimate=pl.CostEstimate(
            flops=6 * rows_all * ff * width, bytes_accessed=30000000, transcendentals=0
        ),
    )(slot_row, hidden, comb, grad, w)


def per_device(gate_pre, up_pre, out_grad, combine, expert_ids, down_weight):
    tokens = gate_pre.shape[0]
    width = down_weight.shape[2]
    flat = jnp.concatenate([expert_ids[:, 0], expert_ids[:, 1]])
    onehot = (flat[:, None] == jnp.arange(E, dtype=jnp.int32)[None, :]).astype(BF16)
    count = tokens * TOP
    before = (jnp.arange(count)[:, None] > jnp.arange(count)[None, :]).astype(BF16)
    earlier = jnp.dot(before, onehot, preferred_element_type=F32)
    position = jnp.sum(earlier * onehot.astype(F32), axis=1).astype(jnp.int32)
    slot_row = (flat * CAP + position).reshape(1, count)

    gate_f = gate_pre.astype(F32)
    up_f = up_pre.astype(F32)
    sig = jax.nn.sigmoid(gate_f)
    hidden = (gate_f * sig * up_f).astype(BF16)
    mixed, hg, wg, cg = exchange(
        slot_row, jnp.transpose(hidden, (1, 0, 2)), combine.T, out_grad, down_weight[0]
    )
    combine_grad = cg.T
    hidden_grad = jnp.transpose(hg, (1, 0, 2))
    gate_grad = (hidden_grad * up_f * sig * (1.0 + gate_f * (1.0 - sig))).astype(BF16)
    up_grad = (hidden_grad * gate_f * sig).astype(BF16)
    return mixed, combine_grad, gate_grad, up_grad, wg[None]


def solution(mesh):
    return jax.shard_map(
        per_device,
        mesh=mesh,
        in_specs=(
            P("dp", None, "hid"),
            P("dp", None, "hid"),
            P("dp", None),
            P("dp", None),
            P("dp", None),
            P("dp", "hid", None),
        ),
        out_specs=(
            P("dp", None, "hid"),
            P("dp", None),
            P("dp", None, "hid"),
            P("dp", None, "hid"),
            P("dp", "hid", None),
        ),
        check_vma=False,
    )
```
